256 devices in a mesh: blk: 64 (over y, x, z_hi), rows: 4 (over z_lo, core).
Axes of the slice: x: 4, y: 4, z: 8 (z_hi: 4, z_lo: 2; z = z_hi * 2 + z_lo), core: 2. Of those that a mesh axis runs over, the one named last changes fastest.
Arguments:
- sens_tiles: bfloat16 [16384, 512, 128], P('blk', 'rows'), may hold values from -1 to 1
- start_basis: bfloat16 [64, 262144], P(None, 'blk'), may hold values from -6 to 6
- row_blocks: int32 [16384, 4], P('blk', 'rows'), may hold values from 0 to 7, as said below
- col_blocks: int32 [16384, 4], P('blk', 'rows'), may hold values from 0 to 31, as said below
- live_counts: int32 [64, 4], P('blk', 'rows'), may hold values from 64 to 256, as said below
Outputs:
- orthonormal: float32 [4, 64, 262144], P(None, None, ('blk', 'rows'))
The draws below stay inside these ranges and needn't reach their ends.
Inputs may be any that keep to these rules, and one draw needn't show every extreme that they name: Within one device the pairs (row_blocks, col_blocks) of its 256 slots are distinct. Within one device the pairs (row_blocks, col_blocks) of its 256 slots are distinct. Slots 0 to live_counts - 1 of a device hold its tiles; some device has all 256 slots live.
All inputs are finite; a program needn't handle non-finite values.
Results may differ from the reference program's by a relative error of at most 0.012.
The reference program's roundings to bfloat16 on the way count: a program that leaves them out, or rounds other values in their place, can miss the bound.
Values may be sent and summed in bfloat16 or wider, within the bound.
No kernel may reach another device: no remote copies, remote signals or barrier semaphores. Data moves between devices by JAX's collectives and lax.ppermute only.
A program may use at most 128 MiB of HBM per device.

```python
import math
import jax
import jax.numpy as jnp
from jax import lax

TILE = 128
K = 64
RB = 8
CB = 32
MAXB = 256
ITERS = 4
DATA = 4096
CELLS = 262144
SLOTS = 16384
N_BLK = 64
N_ROWS = 4


grade_span = 3.28


def pattern_pairs(key):
    base = jax.random.fold_in(key, 7)
    keys = jax.random.split(base, N_BLK * N_ROWS)
    orders = jax.vmap(lambda single: jax.random.permutation(single, RB * CB))(keys)[:, :MAXB]
    rows_part = (orders // CB).reshape(N_BLK, N_ROWS, MAXB).transpose(0, 2, 1).reshape(N_BLK * MAXB, N_ROWS)
    cols_part = (orders % CB).reshape(N_BLK, N_ROWS, MAXB).transpose(0, 2, 1).reshape(N_BLK * MAXB, N_ROWS)
    return (rows_part.astype(jnp.int32), cols_part.astype(jnp.int32))


def draw_sens_tiles(key, part):
    rows_part = pattern_pairs(key)[0]
    datum_block = jnp.arange(N_ROWS, dtype=jnp.int32)[None, :] * RB + rows_part
    datum_index = datum_block[:, :, None] * TILE + jnp.arange(TILE, dtype=jnp.int32)[None, None, :]
    ranking = jax.random.permutation(jax.random.fold_in(key, 13), DATA)
    levels = jnp.minimum(ranking, K).astype(jnp.float32) / K
    weights = jnp.exp(-grade_span * levels)
    row_scale = jnp.take(weights, datum_index.reshape(-1)).reshape(SLOTS, N_ROWS * TILE)
    noise_key = jax.random.fold_in(key, 17)
    values = jax.random.truncated_normal(noise_key, -6.0, 6.0, (SLOTS, N_ROWS * TILE, TILE), jnp.float32)
    return (values * (row_scale[:, :, None] / math.sqrt(TILE))).astype(jnp.bfloat16)


def draw_row_blocks(key, part):
    return pattern_pairs(key)[0]


def draw_col_blocks(key, part):
    return pattern_pairs(key)[1]


def draw_live_counts(key, part):
    base = jax.random.fold_in(key, 11)
    first, second = jax.random.split(base)
    divisor = jax.random.randint(first, (N_BLK * N_ROWS,), 1, 5)
    counted = MAXB // divisor
    fullest = jax.random.randint(second, (), 0, N_BLK * N_ROWS)
    counted = jnp.where(jnp.arange(N_BLK * N_ROWS) == fullest, MAXB, counted)
    return counted.reshape(N_BLK, N_ROWS).astype(jnp.int32)


def steps_of(rng, shape, shards, smallest, top_value):
    gain, own = 1.0, jax.random.fold_in(rng, 6)
    for position, parts in shards:
        draws = jnp.exp(jax.random.uniform(jax.random.fold_in(own, position), (parts,), jnp.float32, smallest / len(shards), top_value / len(shards)))
        gain = gain * jnp.repeat(draws, shape[position] // parts).reshape([-1 if axis == position else 1 for axis in range(len(shape))])
    return gain


def scatter_about(own_key, extent, deviation, reach, cuts=(), kind=jnp.bfloat16):
    values = deviation * jax.random.normal(own_key, extent, jnp.float32)
    if cuts:
        values = values * steps_of(own_key, extent, cuts, -0.22, 0.18)
    return jnp.clip(values, -reach, reach).astype(kind)


def setup_inputs(seed: int = 0) -> dict:
    arg_keys = jax.random.split(jax.random.key(seed), 6)
    sens_tiles = draw_sens_tiles(jax.random.fold_in(arg_keys[5], 71), 0)
    start_basis = scatter_about(arg_keys[1], (K, CELLS), 1.0, 6.0, ((1, 64),))
    row_blocks = draw_row_blocks(jax.random.fold_in(arg_keys[5], 71), 0)
    col_blocks = draw_col_blocks(jax.random.fold_in(arg_keys[5], 71), 0)
    live_counts = draw_live_counts(jax.random.fold_in(arg_keys[5], 71), 0)
    return {"sens_tiles": sens_tiles, "start_basis": start_basis, "row_blocks": row_blocks, "col_blocks": col_blocks, "live_counts": live_counts}


def forward_one(tile_set, basis_blocks, row_slots, col_slots, count_live):
    picked = jnp.take(basis_blocks, col_slots, axis=1)
    products = jnp.einsum('kst,sit->ksi', picked, tile_set)
    live = jnp.arange(MAXB) < count_live
    onehot = ((row_slots[None, :] == jnp.arange(RB)[:, None]) & live[None, :]).astype(jnp.float32)
    summed = jnp.einsum('ksi,rs->kri', products, onehot, precision=lax.Precision.HIGHEST)
    return summed.reshape(K, RB * TILE)

def backward_one(tile_set, image_blocks, row_slots, col_slots, count_live):
    picked = jnp.take(image_blocks, row_slots, axis=1)
    products = jnp.einsum('ksi,sij->ksj', picked, tile_set)
    live = jnp.arange(MAXB) < count_live
    onehot = ((col_slots[None, :] == jnp.arange(CB)[:, None]) & live[None, :]).astype(jnp.float32)
    summed = jnp.einsum('ksj,cs->kcj', products, onehot, precision=lax.Precision.HIGHEST)
    return summed.reshape(K, CB * TILE)

def cholesky_qr(current, total):
    gram = jnp.dot(current, current.T, precision=lax.Precision.HIGHEST) / total
    lower = jnp.linalg.cholesky(gram)
    return jax.scipy.linalg.solve_triangular(lower, current, lower=True)

def reference(sens_tiles, start_basis, row_blocks, col_blocks, live_counts):
    tile_grid = sens_tiles.reshape(N_BLK, MAXB, N_ROWS, TILE, TILE)
    row_grid = row_blocks.reshape(N_BLK, MAXB, N_ROWS)
    col_grid = col_blocks.reshape(N_BLK, MAXB, N_ROWS)
    total = float(N_BLK * CB * TILE)
    basis_now = start_basis
    results = []
    for iteration in range(ITERS):
        blocks = basis_now.astype(jnp.float32).reshape(K, N_BLK, CB, TILE)

        def add_block(accum, index):
            tile_set = tile_grid[index].astype(jnp.float32)
            own = blocks[:, index]
            terms = jax.vmap(lambda place: forward_one(tile_set[:, place], own, row_grid[index, :, place], col_grid[index, :, place], live_counts[index, place]))(jnp.arange(N_ROWS))
            return (accum + terms, None)
        image, unused = lax.scan(add_block, jnp.zeros((N_ROWS, K, RB * TILE), jnp.float32), jnp.arange(N_BLK))
        image_half = image.astype(jnp.bfloat16)
        image_float = image_half.astype(jnp.float32).reshape(N_ROWS, K, RB, TILE)

        def back_block(index):
            tile_set = tile_grid[index].astype(jnp.float32)
            terms = jax.vmap(lambda place: backward_one(tile_set[:, place], image_float[place], row_grid[index, :, place], col_grid[index, :, place], live_counts[index, place]))(jnp.arange(N_ROWS))
            return jnp.sum(terms, axis=0)
        hessian = lax.map(back_block, jnp.arange(N_BLK))
        hessian = jnp.transpose(hessian, (1, 0, 2)).reshape(K, N_BLK * CB * TILE)
        result = cholesky_qr(hessian, total)
        results.append(result)
        basis_now = result.astype(jnp.bfloat16)
    return jnp.stack(results, axis=0)
```

```python
import jax
import jax.numpy as jnp
from jax import lax
from jax.experimental import pallas as pl
from jax.experimental.pallas import tpu as pltpu
from jax.sharding import Mesh
from jax.sharding import PartitionSpec as P

TILE = 128
K = 64
RB = 8
CB = 32
MAXB = 256
ITERS = 4
CELLS = 262144.0
WIDTH = CB * TILE
HEIGHT = RB * TILE
HALF = WIDTH // 2
OWN = WIDTH // 4
PEERS = 16
EACH = 5

f32 = jnp.float32
bf16 = jnp.bfloat16
BLK = ("y", "x", "h")
ROWS = ("l", "c")
PLANE = ("y", "x")
VMEM = pl.BlockSpec(memory_space=pltpu.VMEM)
SMEM = pl.BlockSpec(memory_space=pltpu.SMEM)
HBM = pl.BlockSpec(memory_space=pl.ANY)


def dot_rows(a, b):
    return lax.dot_general(a, b, (((1,), (1,)), ((), ())), preferred_element_type=f32)


def params(mib):
    return pltpu.CompilerParams(vmem_limit_bytes=mib << 20)


def write_packed(out, image, gram):
    for n in range(PEERS * EACH):
        rows = pl.ds((n % EACH) * 8, 8)
        if n < 64:
            g, j = divmod(n, 8)
            out[n // EACH, rows, :] = image[g * 8 : g * 8 + 8, j * TILE : (j + 1) * TILE]
        elif n < 72 and gram is not None:
            g = n - 64
            out[n // EACH, rows, :] = gram[g * 8 : g * 8 + 8, :]
        else:
            out[n // EACH, rows, :] = jnp.zeros((8, TILE), f32)


def read_packed(packed, n):
    return packed[n // EACH, pl.ds((n % EACH) * 8, 8), :]


def two_parts(x):
    high = x.astype(bf16)
    low = (x - high.astype(f32)).astype(bf16)
    return jnp.concatenate([high, low], axis=0)


def gram_of(parts):
    four = dot_rows(parts, parts)
    two = four[:K] + four[K:]
    return two[:, :K] + two[:, K:]


def inverse_factor(gram):
    row = lax.broadcasted_iota(jnp.int32, (K, K), 0)
    col = lax.broadcasted_iota(jnp.int32, (K, K), 1)
    work = jnp.concatenate([gram, (row == col).astype(f32)], axis=1)
    below = lax.broadcasted_iota(jnp.int32, (K, 2 * K), 0)
    scale = jnp.zeros((K, 1), f32)
    for k in range(K):
        pivot_row = work[k : k + 1, :]
        column = work[:, k : k + 1]
        pivot = work[k : k + 1, k : k + 1]
        factor = jnp.where(below[:, :1] > k, column * (1.0 / pivot), 0.0)
        scale = jnp.where(below[:, :1] == k, lax.rsqrt(pivot), scale)
        work = work - factor * pivot_row
    return work[:, K:] * scale


def start_kernel(place, live, tiles, basis, turn, dense, packed, nothing, sem):
    nothing[...] = jnp.zeros_like(nothing)

    def put(s, carry):
        at = place[s]
        window = dense.at[
            pl.ds(pl.multiple_of((at // CB) * TILE, TILE), TILE),
            pl.ds(pl.multiple_of((at % CB) * TILE, TILE), TILE),
        ]

        @pl.when(s < live[0])
        def _():
            pltpu.make_async_copy(tiles.at[s], window, sem).start()

        @pl.when(s >= live[0])
        def _():
            pltpu.make_async_copy(nothing, window, sem).start()

        return carry

    lax.fori_loop(0, MAXB, put, 0)
    pltpu.make_async_copy(dense, dense, sem).wait()
    core = turn[0]
    image = jnp.zeros((K, HEIGHT), f32)
    for p in range(4):
        q = (p % 2) * 2 + ((p // 2) ^ core)
        part = basis[:, pl.ds(pl.multiple_of(q * OWN, OWN), OWN)]
        image = image + dot_rows(part, dense[:, p * OWN : (p + 1) * OWN])
    write_packed(packed, image, None)


def forward_kernel(mine, other, dense, packed):
    image = jnp.zeros((2 * K, HEIGHT), f32)
    grams = []
    for p, half in enumerate((mine, other)):
        parts = two_parts(half[...])
        grams.append(gram_of(parts))
        image = image + dot_rows(parts, dense[:, p * HALF : (p + 1) * HALF])
    gram = grams[0] + grams[1]
    write_packed(packed, image[:K] + image[K:], jnp.concatenate([gram, gram], axis=1))


def gram_kernel(mine, other, out):
    out[...] = gram_of(two_parts(mine[...])) + gram_of(two_parts(other[...]))


def image_of(packed):
    return jnp.concatenate(
        [jnp.concatenate([read_packed(packed, g * 8 + j) for j in range(8)], axis=1) for g in range(8)],
        axis=0,
    )


def spread(image_half, dense, mine, other):
    for n in range(8):
        width = WIDTH // 8
        product = jnp.dot(image_half, dense[:, n * width : (n + 1) * width], preferred_element_type=f32)
        target = mine if n < 4 else other
        target[:, (n % 4) * width : (n % 4 + 1) * width] = product


def first_backward_kernel(packed, dense, mine, other):
    spread(image_of(packed).astype(bf16), dense, mine, other)


def backward_kernel(packed, dense, mine, other, inverse):
    gram = jnp.concatenate([read_packed(packed, 64 + g) for g in range(8)], axis=0)[:, :K]
    found = inverse_factor(gram * (1.0 / CELLS))
    inverse[...] = found
    image = jnp.dot(found, image_of(packed), precision=lax.Precision.HIGHEST, preferred_element_type=f32)
    spread(image.astype(bf16), dense, mine, other)


def finish_kernel(turn, gram, *refs):
    halves, inverses, out = refs[:ITERS], refs[ITERS:-1], refs[-1]
    own = pl.ds(pl.multiple_of(turn[1] * OWN, OWN), OWN)
    last = inverse_factor(gram[...] * (1.0 / CELLS))
    for i in range(ITERS):
        found = inverses[i][...] if i < ITERS - 1 else last
        out[i] = jnp.dot(found, halves[i][:, own], precision=lax.Precision.HIGHEST, preferred_element_type=f32)


def shifted(x, axis, by):
    count = lax.axis_size(axis)
    return lax.ppermute(x, axis, [(i, (i + by) % count) for i in range(count)])


def summed_along(x, axis):
    one, two, three = (shifted(x, axis, by) for by in (1, 2, 3))
    return (x + two) + (one + three)


def summed_over_blk(packed):
    shares = lax.all_to_all(packed, PLANE, 0, 0, tiled=True)
    total = summed_along(jnp.sum(shares, axis=0), "h")
    return lax.all_to_all(jnp.broadcast_to(total[None], packed.shape), PLANE, 0, 0, tiled=True)


def summed_over_rows(mine, other):
    mine = mine + shifted(other, "c", 1)
    mine = mine + shifted(mine, "l", 1)
    return mine, shifted(mine, "c", 1)


def local(sens_tiles, start_basis, row_blocks, col_blocks, live_counts):
    core, low = lax.axis_index("c"), lax.axis_index("l")
    turn = jnp.stack([core, low]).astype(jnp.int32)
    quarter, rest = col_blocks[:, 0] // (CB // 4), col_blocks[:, 0] % (CB // 4)
    position = (((quarter % 2) ^ core) * 2 + quarter // 2) * (CB // 4) + rest
    place = row_blocks[:, 0] * CB + position
    packed_shape = jax.ShapeDtypeStruct((PEERS, EACH * 8, TILE), f32)
    half_shape = jax.ShapeDtypeStruct((K, HALF), f32)
    square_shape = jax.ShapeDtypeStruct((K, K), f32)
    dense, packed = pl.pallas_call(
        start_kernel,
        out_shape=(jax.ShapeDtypeStruct((HEIGHT, WIDTH), bf16), packed_shape),
        in_specs=[SMEM, SMEM, HBM, VMEM, SMEM],
        out_specs=(VMEM, VMEM),
        scratch_shapes=[pltpu.VMEM((TILE, TILE), bf16), pltpu.SemaphoreType.DMA],
        compiler_params=params(20),
    )(place, live_counts[0], sens_tiles, start_basis, turn)
    halves, inverses = [], []
    for iteration in range(ITERS):
        packed = summed_over_blk(packed)
        if iteration == 0:
            mine, other = pl.pallas_call(
                first_backward_kernel,
                out_shape=(half_shape, half_shape),
                in_specs=[VMEM, VMEM],
                out_specs=(VMEM, VMEM),
                compiler_params=params(20),
            )(packed, dense)
        else:
            mine, other, inverse = pl.pallas_call(
                backward_kernel,
                out_shape=(half_shape, half_shape, square_shape),
                in_specs=[VMEM, VMEM],
                out_specs=(VMEM, VMEM, VMEM),
                compiler_params=params(20),
            )(packed, dense)
            inverses.append(inverse)
        mine, other = summed_over_rows(mine, other)
        halves.append(mine)
        if iteration < ITERS - 1:
            packed = pl.pallas_call(
                forward_kernel,
                out_shape=packed_shape,
                in_specs=[VMEM, VMEM, VMEM],
                out_specs=VMEM,
                compiler_params=params(24),
            )(mine, other, dense)
    gram = pl.pallas_call(
        gram_kernel,
        out_shape=square_shape,
        in_specs=[VMEM, VMEM],
        out_specs=VMEM,
        compiler_params=params(12),
    )(mine, other)
    for axis in BLK:
        gram = summed_along(gram, axis)
    return pl.pallas_call(
        finish_kernel,
        out_shape=jax.ShapeDtypeStruct((ITERS, K, OWN), f32),
        in_specs=[SMEM] + [VMEM] * (2 * ITERS),
        out_specs=VMEM,
        compiler_params=params(12),
    )(turn, gram, *halves, *inverses)


def solution(mesh):
    fine = Mesh(mesh.devices.reshape(4, 4, 4, 2, 2), BLK + ROWS)
    in_specs = (
        P(BLK, ROWS, None),
        P(None, BLK),
        P(BLK, ROWS),
        P(BLK, ROWS),
        P(BLK, ROWS),
    )
    out_specs = P(None, None, BLK + ROWS)
    return jax.shard_map(local, mesh=fine, in_specs=in_specs, out_specs=out_specs, check_vma=False)
```

```python
import jax
import jax.numpy as jnp
from jax import lax
from jax.experimental import pallas as pl
from jax.experimental.pallas import tpu as pltpu
from jax.sharding import Mesh
from jax.sharding import PartitionSpec as P

TILE = 128
K = 64
RB = 8
CB = 32
MAXB = 256
ITERS = 4
CELLS = 262144.0
WIDTH = CB * TILE
HEIGHT = RB * TILE
HALF = WIDTH // 2
OWN = WIDTH // 4
PEERS = 16
EACH = 5
PANEL = 4
BATCHES = 8
BATCH = MAXB // BATCHES

f32 = jnp.float32
bf16 = jnp.bfloat16
BLK = ("y", "x", "h")
ROWS = ("l", "c")
PLANE = ("y", "x")
VMEM = pl.BlockSpec(memory_space=pltpu.VMEM)
SMEM = pl.BlockSpec(memory_space=pltpu.SMEM)
HBM = pl.BlockSpec(memory_space=pltpu.HBM)


def dot_rows(a, b):
    return lax.dot_general(a, b, (((1,), (1,)), ((), ())), preferred_element_type=f32)


def params(mib):
    return pltpu.CompilerParams(vmem_limit_bytes=mib << 20)


def write_packed(out, image, gram):
    for n in range(PEERS * EACH):
        rows = pl.ds((n % EACH) * 8, 8)
        if n < 64:
            g, j = divmod(n, 8)
            out[n // EACH, rows, :] = image[g * 8 : g * 8 + 8, j * TILE : (j + 1) * TILE]
        elif n < 72 and gram is not None:
            g = n - 64
            out[n // EACH, rows, :] = gram[g * 8 : g * 8 + 8, :]
        else:
            out[n // EACH, rows, :] = jnp.zeros((8, TILE), f32)


def read_packed(packed, n):
    return packed[n // EACH, pl.ds((n % EACH) * 8, 8), :]


def two_parts(x):
    high = x.astype(bf16)
    low = (x - high.astype(f32)).astype(bf16)
    return jnp.concatenate([high, low], axis=0)


def gram_of(parts):
    four = dot_rows(parts, parts)
    two = four[:K] + four[K:]
    return two[:, :K] + two[:, K:]


def reciprocal(x):
    near = pl.reciprocal(x, approx=True)
    near = near * (2.0 - x * near)
    return near * (2.0 - x * near)


def inverse_factor(gram):
    shape = (K, 2 * K)
    row = lax.broadcasted_iota(jnp.int32, shape, 0)
    col = lax.broadcasted_iota(jnp.int32, shape, 1)
    work = jnp.concatenate([gram, (row[:, :K] == col[:, :K]).astype(f32)], axis=1)
    for k in range(0, K, PANEL):
        columns = [jnp.broadcast_to(work[:, k + j : k + j + 1], shape) for j in range(PANEL)]
        lines = [work[k + j : k + j + 1, :] for j in range(PANEL)]
        for j in range(PANEL):
            at = k + j
            inverse = reciprocal(columns[j][at : at + 1, :])
            factor = jnp.where(row > at, columns[j] * inverse, 0.0)
            for later in range(j + 1, PANEL):
                columns[later] = columns[later] - factor * columns[later][at : at + 1, :]
                to = k + later
                lines[later] = lines[later] - factor[to : to + 1, :] * lines[j]
            work = work - factor * lines[j]
    diagonal = jnp.sum(jnp.where(row == col, work, 0.0), axis=1, keepdims=True)
    return work[:, K:] * lax.rsqrt(diagonal)


def load(dense, held, sems):
    copies = []
    for p in range(4):
        span = pl.ds(p * OWN, OWN)
        copies.append(pltpu.make_async_copy(dense.at[:, span], held.at[:, span], sems.at[p]))
        copies[-1].start()
    return copies


def start_kernel(row_blocks, col_blocks, live, turn, tiles, basis, dense, packed, stock, first, held, sems, first_sem, out_sem):
    get_basis = pltpu.make_async_copy(basis, first, first_sem)
    get_basis.start()
    copies = []
    for n in range(BATCHES):
        span = pl.ds(n * BATCH, BATCH)
        copies.append(pltpu.make_async_copy(tiles.at[span], stock.at[span], sems.at[n]))
        copies[-1].start()
    core, count = turn[0], live[0]

    def window(s):
        col = col_blocks[s]
        quarter = col // (CB // 4)
        position = (((quarter % 2) ^ core) * 2 + quarter // 2) * (CB // 4) + col % (CB // 4)
        return (
            pl.ds(pl.multiple_of(row_blocks[s] * TILE, TILE), TILE),
            pl.ds(pl.multiple_of(position * TILE, TILE), TILE),
        )

    def put(s, carry):
        held[window(s)] = stock[s]
        return carry

    def clear(s, carry):
        held[window(s)] = jnp.zeros((TILE, TILE), bf16)
        return carry

    for n in range(BATCHES):
        copies[n].wait()
        middle = jnp.clip(count, n * BATCH, (n + 1) * BATCH)
        lax.fori_loop(n * BATCH, middle, put, 0)
        lax.fori_loop(middle, (n + 1) * BATCH, clear, 0)
    away = pltpu.make_async_copy(held, dense, out_sem)
    away.start()
    get_basis.wait()
    image = jnp.zeros((K, HEIGHT), f32)
    for p in range(4):
        q = (p % 2) * 2 + ((p // 2) ^ core)
        part = first[:, pl.ds(pl.multiple_of(q * OWN, OWN), OWN)]
        image = image + dot_rows(part, held[:, p * OWN : (p + 1) * OWN])
    write_packed(packed, image, None)
    away.wait()


def forward_kernel(mine, other, dense, packed, held, sems):
    copies = load(dense, held, sems)
    image = jnp.zeros((2 * K, HEIGHT), f32)
    grams = []
    for p, half in enumerate((mine, other)):
        parts = two_parts(half[...])
        grams.append(gram_of(parts))
        for n in range(2):
            q = p * 2 + n
            copies[q].wait()
            image = image + dot_rows(parts[:, n * OWN : (n + 1) * OWN], held[:, q * OWN : (q + 1) * OWN])
    gram = grams[0] + grams[1]
    write_packed(packed, image[:K] + image[K:], jnp.concatenate([gram, gram], axis=1))


def gram_kernel(own, out):
    gram = gram_of(two_parts(own[...]))
    out[...] = jnp.concatenate([gram[: K // 2], gram[K // 2 :]], axis=1)


def image_of(packed):
    return jnp.concatenate(
        [jnp.concatenate([read_packed(packed, g * 8 + j) for j in range(8)], axis=1) for g in range(8)],
        axis=0,
    )


def spread(image_half, copies, held, mine, other):
    for p in range(4):
        copies[p].wait()
        target = mine if p < 2 else other
        for n in range(2):
            source = pl.ds(p * OWN + n * OWN // 2, OWN // 2)
            product = jnp.dot(image_half, held[:, source], preferred_element_type=f32)
            target[:, pl.ds((p % 2) * OWN + n * OWN // 2, OWN // 2)] = product


def first_backward_kernel(packed, dense, mine, other, held, sems):
    copies = load(dense, held, sems)
    spread(image_of(packed).astype(bf16), copies, held, mine, other)


def backward_kernel(packed, dense, mine, other, inverse, held, sems):
    copies = load(dense, held, sems)
    gram = jnp.concatenate([read_packed(packed, 64 + g) for g in range(8)], axis=0)[:, :K]
    found = inverse_factor(gram * (1.0 / CELLS))
    inverse[...] = found
    image = jnp.dot(found, image_of(packed), precision=lax.Precision.HIGHEST, preferred_element_type=f32)
    spread(image.astype(bf16), copies, held, mine, other)


def finish_kernel(turn, gram, *refs):
    halves, inverses, out = refs[:ITERS], refs[ITERS:-1], refs[-1]
    own = pl.ds(pl.multiple_of(turn[1] * OWN, OWN), OWN)
    whole = jnp.concatenate([gram[:, :K], gram[:, K:]], axis=0)
    last = inverse_factor(whole * (1.0 / CELLS))
    for i in range(ITERS):
        found, taken = (inverses[i][...], halves[i][:, own]) if i < ITERS - 1 else (last, halves[i][...])
        out[i] = jnp.dot(found, taken, precision=lax.Precision.HIGHEST, preferred_element_type=f32)


def shifted(x, axis, by):
    count = lax.axis_size(axis)
    return lax.ppermute(x, axis, [(i, (i + by) % count) for i in range(count)])


def summed_by_all(x, axes):
    count = lax.axis_size(axes)
    return jnp.sum(lax.all_to_all(jnp.broadcast_to(x[None], (count, *x.shape)), axes, 0, 0, tiled=True), axis=0)


def summed_over_blk(packed):
    shares = lax.all_to_all(packed, PLANE, 0, 0, tiled=True)
    total = summed_by_all(jnp.sum(shares, axis=0), "h")
    return lax.all_to_all(jnp.broadcast_to(total[None], packed.shape), PLANE, 0, 0, tiled=True)


def local(sens_tiles, start_basis, row_blocks, col_blocks, live_counts):
    core, low = lax.axis_index("c"), lax.axis_index("l")
    turn = jnp.stack([core, low]).astype(jnp.int32)
    packed_shape = jax.ShapeDtypeStruct((PEERS, EACH * 8, TILE), f32)
    half_shape = jax.ShapeDtypeStruct((K, HALF), f32)
    square_shape = jax.ShapeDtypeStruct((K, K), f32)
    dense_shape = jax.ShapeDtypeStruct((HEIGHT, WIDTH), bf16)
    holding = [pltpu.VMEM((HEIGHT, WIDTH), bf16), pltpu.SemaphoreType.DMA((4,))]
    dense, packed = pl.pallas_call(
        start_kernel,
        out_shape=(dense_shape, packed_shape),
        in_specs=[SMEM, SMEM, SMEM, SMEM, HBM, HBM],
        out_specs=(HBM, VMEM),
        scratch_shapes=[
            pltpu.VMEM(sens_tiles.shape, bf16),
            pltpu.VMEM(start_basis.shape, bf16),
            pltpu.VMEM((HEIGHT, WIDTH), bf16),
            pltpu.SemaphoreType.DMA((BATCHES,)),
            pltpu.SemaphoreType.DMA,
            pltpu.SemaphoreType.DMA,
        ],
        compiler_params=params(57),
    )(row_blocks.reshape(MAXB), col_blocks.reshape(MAXB), live_counts.reshape(1), turn, sens_tiles, start_basis)
    halves, inverses = [], []
    for iteration in range(ITERS):
        packed = summed_over_blk(packed)
        first = iteration == 0
        mine, other, *inverse = pl.pallas_call(
            first_backward_kernel if first else backward_kernel,
            out_shape=(half_shape, half_shape) if first else (half_shape, half_shape, square_shape),
            in_specs=[VMEM, HBM],
            out_specs=(VMEM, VMEM) if first else (VMEM, VMEM, VMEM),
            scratch_shapes=holding,
            compiler_params=params(50),
        )(packed, dense)
        inverses += inverse
        mine = mine + shifted(other, "c", 1)
        if iteration == ITERS - 1:
            kept = lax.dynamic_slice_in_dim(mine, low * OWN, OWN, 1)
            sent = lax.dynamic_slice_in_dim(mine, (1 - low) * OWN, OWN, 1)
            halves.append(kept + shifted(sent, "l", 1))
            break
        mine = mine + shifted(mine, "l", 1)
        halves.append(mine)
        packed = pl.pallas_call(
            forward_kernel,
            out_shape=packed_shape,
            in_specs=[VMEM, VMEM, HBM],
            out_specs=VMEM,
            scratch_shapes=holding,
            compiler_params=params(50),
        )(mine, shifted(mine, "c", 1), dense)
    gram = pl.pallas_call(
        gram_kernel,
        out_shape=jax.ShapeDtypeStruct((K // 2, 2 * K), f32),
        in_specs=[VMEM],
        out_specs=VMEM,
        compiler_params=params(50),
    )(halves[-1])
    gram = summed_by_all(summed_by_all(gram, PLANE + ("c",)), ("h", "l"))
    return pl.pallas_call(
        finish_kernel,
        out_shape=jax.ShapeDtypeStruct((ITERS, K, OWN), f32),
        in_specs=[SMEM] + [VMEM] * (2 * ITERS),
        out_specs=VMEM,
        compiler_params=params(50),
    )(turn, gram, *halves, *inverses)


def solution(mesh):
    fine = Mesh(mesh.devices.reshape(4, 4, 4, 2, 2), BLK + ROWS)
    in_specs = (
        P(BLK, ROWS, None),
        P(None, BLK),
        P(BLK, ROWS),
        P(BLK, ROWS),
        P(BLK, ROWS),
    )
    out_specs = P(None, None, BLK + ROWS)
    return jax.shard_map(local, mesh=fine, in_specs=in_specs, out_specs=out_specs, check_vma=False)
```

```python
import jax
import jax.numpy as jnp
from jax import lax
from jax.experimental import pallas as pl
from jax.experimental.pallas import tpu as pltpu
from jax.sharding import Mesh
from jax.sharding import PartitionSpec as P

TILE = 128
K = 64
RB = 8
CB = 32
MAXB = 256
ITERS = 4
CELLS = 262144.0
WIDTH = CB * TILE
HEIGHT = RB * TILE
HALF = WIDTH // 2
OWN = WIDTH // 4
PEERS = 16
EACH = 5
PANEL = 4
START_MIB = 40
BATCHES = 8
BATCH = MAXB // BATCHES

f32 = jnp.float32
bf16 = jnp.bfloat16
BLK = ("y", "x", "h")
ROWS = ("l", "c")
PLANE = ("y", "x")
VMEM = pl.BlockSpec(memory_space=pltpu.VMEM)
SMEM = pl.BlockSpec(memory_space=pltpu.SMEM)
HBM = pl.BlockSpec(memory_space=pltpu.HBM)


def dot_rows(a, b):
    return lax.dot_general(a, b, (((1,), (1,)), ((), ())), preferred_element_type=f32)


def params(mib):
    return pltpu.CompilerParams(vmem_limit_bytes=mib << 20)


def write_packed(out, image, gram):
    for n in range(PEERS * EACH):
        rows = pl.ds((n % EACH) * 8, 8)
        if n < 64:
            g, j = divmod(n, 8)
            out[n // EACH, rows, :] = image[g * 8 : g * 8 + 8, j * TILE : (j + 1) * TILE]
        elif n < 72 and gram is not None:
            g = n - 64
            out[n // EACH, rows, :] = gram[g * 8 : g * 8 + 8, :]
        else:
            out[n // EACH, rows, :] = jnp.zeros((8, TILE), f32)


def read_packed(packed, n):
    return packed[n // EACH, pl.ds((n % EACH) * 8, 8), :]


def two_parts(x):
    high = x.astype(bf16)
    low = (x - high.astype(f32)).astype(bf16)
    return jnp.concatenate([high, low], axis=0)


def gram_of(parts):
    four = dot_rows(parts, parts)
    two = four[:K] + four[K:]
    return two[:, :K] + two[:, K:]


def reciprocal(x):
    near = pl.reciprocal(x, approx=True)
    near = near * (2.0 - x * near)
    return near * (2.0 - x * near)


def inverse_factor(gram):
    shape = (K, 2 * K)
    row = lax.broadcasted_iota(jnp.int32, shape, 0)
    col = lax.broadcasted_iota(jnp.int32, shape, 1)
    work = jnp.concatenate([gram, (row[:, :K] == col[:, :K]).astype(f32)], axis=1)
    for k in range(0, K, PANEL):
        columns = [jnp.broadcast_to(work[:, k + j : k + j + 1], shape) for j in range(PANEL)]
        lines = [work[k + j : k + j + 1, :] for j in range(PANEL)]
        for j in range(PANEL):
            at = k + j
            inverse = reciprocal(columns[j][at : at + 1, :])
            factor = jnp.where(row > at, columns[j] * inverse, 0.0)
            for later in range(j + 1, PANEL):
                columns[later] = columns[later] - factor * columns[later][at : at + 1, :]
                to = k + later
                lines[later] = lines[later] - factor[to : to + 1, :] * lines[j]
            work = work - factor * lines[j]
    diagonal = jnp.sum(jnp.where(row == col, work, 0.0), axis=1, keepdims=True)
    return work[:, K:] * lax.rsqrt(diagonal)


def start_kernel(row_blocks, col_blocks, live, turn, tiles, basis, dense, packed, stock, first, sems, first_sem):
    get_basis = pltpu.make_async_copy(basis, first, first_sem)
    get_basis.start()
    copies = []
    for n in range(BATCHES):
        span = pl.ds(n * BATCH, BATCH)
        copies.append(pltpu.make_async_copy(tiles.at[span], stock.at[span], sems.at[n]))
        copies[-1].start()
    core, count = turn[0], live[0]

    def window(s):
        col = col_blocks[s]
        quarter = col // (CB // 4)
        position = (((quarter % 2) ^ core) * 2 + quarter // 2) * (CB // 4) + col % (CB // 4)
        return (
            pl.ds(pl.multiple_of(row_blocks[s] * TILE, TILE), TILE),
            pl.ds(pl.multiple_of(position * TILE, TILE), TILE),
        )

    def put(s, carry):
        dense[window(s)] = stock[s]
        return carry

    def clear(s, carry):
        dense[window(s)] = jnp.zeros((TILE, TILE), bf16)
        return carry

    for n in range(BATCHES):
        copies[n].wait()
        middle = jnp.clip(count, n * BATCH, (n + 1) * BATCH)
        lax.fori_loop(n * BATCH, middle, put, 0)
        lax.fori_loop(middle, (n + 1) * BATCH, clear, 0)
    get_basis.wait()
    image = jnp.zeros((K, HEIGHT), f32)
    for p in range(4):
        q = (p % 2) * 2 + ((p // 2) ^ core)
        part = first[:, pl.ds(pl.multiple_of(q * OWN, OWN), OWN)]
        image = image + dot_rows(part, dense[:, p * OWN : (p + 1) * OWN])
    write_packed(packed, image, None)


def gathered(chunk, mine, other, dense):
    image, grams = 0.0, []
    for p, half in ((chunk, mine), (2 + chunk, other)):
        parts = two_parts(half[...])
        grams.append(gram_of(parts))
        image = image + dot_rows(parts, dense[:, p * OWN : (p + 1) * OWN])
    return image[:K] + image[K:], grams[0] + grams[1]


def forward_kernel(mine, other, dense, image, gram):
    image[...], gram[...] = gathered(0, mine, other, dense)


def forward_last_kernel(mine, other, dense, image_before, gram_before, packed):
    image, gram = gathered(1, mine, other, dense)
    gram = gram_before[...] + gram
    write_packed(packed, image_before[...] + image, jnp.concatenate([gram, gram], axis=1))


def gram_kernel(own, out):
    gram = gram_of(two_parts(own[...]))
    out[...] = jnp.concatenate([gram[: K // 2], gram[K // 2 :]], axis=1)


def image_of(packed):
    return jnp.concatenate(
        [jnp.concatenate([read_packed(packed, g * 8 + j) for j in range(8)], axis=1) for g in range(8)],
        axis=0,
    )


def spread(chunk, image_half, dense, mine, other):
    for p, target in ((chunk, mine), (2 + chunk, other)):
        for n in range(2):
            width = OWN // 2
            source = pl.ds(p * OWN + n * width, width)
            product = jnp.dot(image_half, dense[:, source], preferred_element_type=f32)
            target[:, n * width : (n + 1) * width] = product


def first_backward_kernel(packed, dense, mine, other, kept):
    kept[...] = image_of(packed).astype(bf16)
    spread(0, kept[...], dense, mine, other)


def backward_kernel(packed, dense, mine, other, kept, inverse):
    gram = jnp.concatenate([read_packed(packed, 64 + g) for g in range(8)], axis=0)[:, :K]
    found = inverse_factor(gram * (1.0 / CELLS))
    inverse[...] = found
    image = jnp.dot(found, image_of(packed), precision=lax.Precision.HIGHEST, preferred_element_type=f32)
    kept[...] = image.astype(bf16)
    spread(0, kept[...], dense, mine, other)


def backward_last_kernel(kept, dense, mine, other):
    spread(1, kept[...], dense, mine, other)


def add_kernel(a, b, out):
    out[...] = a[...] + b[...]


def share_kernel(parts, out):
    total = parts[0]
    for n in range(1, parts.shape[0]):
        total = total + parts[n]
    for n in range(out.shape[0]):
        out[n] = total


def finish_kernel(turn, gram, *refs):
    halves, last_half, inverses, out = refs[: 2 * ITERS - 2], refs[2 * ITERS - 2], refs[2 * ITERS - 1 : -1], refs[-1]
    whole = jnp.concatenate([gram[:, :K], gram[:, K:]], axis=0)
    last = inverse_factor(whole * (1.0 / CELLS))
    for i in range(ITERS):
        if i < ITERS - 1:
            found, taken = inverses[i][...], jnp.where(turn[1] == 0, halves[2 * i][...], halves[2 * i + 1][...])
        else:
            found, taken = last, last_half[...]
        out[i] = jnp.dot(found, taken, precision=lax.Precision.HIGHEST, preferred_element_type=f32)


def shifted(x, axis, by):
    count = lax.axis_size(axis)
    return lax.ppermute(x, axis, [(i, (i + by) % count) for i in range(count)])


def summed_by_all(x, axes):
    count = lax.axis_size(axes)
    return jnp.sum(lax.all_to_all(jnp.broadcast_to(x[None], (count, *x.shape)), axes, 0, 0, tiled=True), axis=0)


def call(kernel, name, mib, ins, outs, arrays, flops=0, scratch=()):
    shapes = tuple(jax.ShapeDtypeStruct(*o) for o in outs)
    moved = sum(a.size * a.dtype.itemsize for a in (*arrays, *shapes))
    found = pl.pallas_call(
        kernel,
        out_shape=shapes,
        in_specs=ins,
        out_specs=(VMEM,) * len(outs),
        scratch_shapes=list(scratch),
        compiler_params=params(mib),
        cost_estimate=pl.CostEstimate(flops=flops, bytes_accessed=moved, transcendentals=0),
        name=name,
    )(*arrays)
    return found[0] if len(outs) == 1 else found


def shared(parts, count):
    return call(share_kernel, "share", 4, [VMEM], [((count, *parts.shape[1:]), f32)], [parts])


def added(a, b):
    return call(add_kernel, "add", 4, [VMEM, VMEM], [(a.shape, f32)], [a, b])


def summed_over_blk(packed):
    shares = lax.all_to_all(packed, PLANE, 0, 0, tiled=True)
    shares = lax.all_to_all(shared(shares, 4), "h", 0, 0, tiled=True)
    return lax.all_to_all(shared(shares, PEERS), PLANE, 0, 0, tiled=True)


def local(sens_tiles, start_basis, row_blocks, col_blocks, live_counts):
    core, low = lax.axis_index("c"), lax.axis_index("l")
    turn = jnp.stack([core, low]).astype(jnp.int32)
    packed_shape = ((PEERS, EACH * 8, TILE), f32)
    chunk, square, kept_shape = ((K, OWN), f32), ((K, K), f32), ((K, HEIGHT), bf16)
    work = 2 * K * HEIGHT * HALF
    dense, packed = call(
        start_kernel,
        "start",
        START_MIB,
        [SMEM, SMEM, SMEM, SMEM, HBM, HBM],
        [((HEIGHT, WIDTH), bf16), packed_shape],
        [row_blocks.reshape(MAXB), col_blocks.reshape(MAXB), live_counts.reshape(1), turn, sens_tiles, start_basis],
        2 * work,
        [
            pltpu.VMEM(sens_tiles.shape, bf16),
            pltpu.VMEM(start_basis.shape, bf16),
            pltpu.SemaphoreType.DMA((BATCHES,)),
            pltpu.SemaphoreType.DMA,
        ],
    )
    halves, inverses = [], []
    for iteration in range(ITERS):
        packed = summed_over_blk(packed)
        if iteration == 0:
            mine, other, kept = call(first_backward_kernel, "backward", 8, [VMEM, VMEM], [chunk, chunk, kept_shape], [packed, dense], work)
        else:
            mine, other, kept, inverse = call(
                backward_kernel, "backward", 8, [VMEM, VMEM], [chunk, chunk, kept_shape, square], [packed, dense], work
            )
            inverses.append(inverse)
        moving = shifted(other, "c", 1)
        mine_last, other_last = call(backward_last_kernel, "backward_last", 8, [VMEM, VMEM], [chunk, chunk], [kept, dense], work)
        mine = added(mine, moving)
        if iteration == ITERS - 1:
            mine_last = added(mine_last, shifted(other_last, "c", 1))
            own = jnp.where(low == 0, mine, mine_last)
            sent = jnp.where(low == 0, mine_last, mine)
            own = own + shifted(sent, "l", 1)
            break
        moving = shifted(mine, "l", 1)
        mine_last = added(mine_last, shifted(other_last, "c", 1))
        moving_last = shifted(mine_last, "l", 1)
        mine, mine_last = lax.optimization_barrier((mine, mine_last))
        mine = added(mine, moving)
        image, gram = call(
            forward_kernel, "forward", 12, [VMEM, VMEM, VMEM], [chunk, square], [mine, shifted(mine, "c", 1), dense], 2 * work
        )
        mine_last = added(mine_last, moving_last)
        packed = call(
            forward_last_kernel,
            "forward_last",
            12,
            [VMEM] * 5,
            [packed_shape],
            [mine_last, shifted(mine_last, "c", 1), dense, image, gram],
            2 * work,
        )
        halves += [mine, mine_last]
    gram = call(gram_kernel, "gram", 50, [VMEM], [((K // 2, 2 * K), f32)], [own])
    gram = summed_by_all(summed_by_all(gram, PLANE + ("c",)), ("h", "l"))
    return call(
        finish_kernel,
        "finish",
        50,
        [SMEM] + [VMEM] * (3 * ITERS - 1),
        [((ITERS, K, OWN), f32)],
        [turn, gram, *halves, own, *inverses],
    )


def solution(mesh):
    fine = Mesh(mesh.devices.reshape(4, 4, 4, 2, 2), BLK + ROWS)
    in_specs = (
        P(BLK, ROWS, None),
        P(None, BLK),
        P(BLK, ROWS),
        P(BLK, ROWS),
        P(BLK, ROWS),
    )
    out_specs = P(None, None, BLK + ROWS)
    return jax.shard_map(local, mesh=fine, in_specs=in_specs, out_specs=out_specs, check_vma=False)
```

```python
import jax
import jax.numpy as jnp
from jax import lax
from jax.experimental import pallas as pl
from jax.experimental.pallas import tpu as pltpu
from jax.sharding import Mesh
from jax.sharding import PartitionSpec as P

TILE = 128
K = 64
RB = 8
CB = 32
MAXB = 256
ITERS = 4
CELLS = 262144.0
WIDTH = CB * TILE
HEIGHT = RB * TILE
HALF = WIDTH // 2
OWN = WIDTH // 4
PEERS = 16
EACH = 5
PANEL = 8
START_MIB = 40
BATCHES = 8
BATCH = MAXB // BATCHES

f32 = jnp.float32
bf16 = jnp.bfloat16
BLK = ("y", "x", "h")
ROWS = ("l", "c")
PLANE = ("y", "x")
VMEM = pl.BlockSpec(memory_space=pltpu.VMEM)
SMEM = pl.BlockSpec(memory_space=pltpu.SMEM)
HBM = pl.BlockSpec(memory_space=pltpu.HBM)


def dot_rows(a, b):
    return lax.dot_general(a, b, (((1,), (1,)), ((), ())), preferred_element_type=f32)


def params(mib):
    return pltpu.CompilerParams(vmem_limit_bytes=mib << 20)


def write_packed(out, image, gram):
    for n in range(PEERS * EACH):
        rows = pl.ds((n % EACH) * 8, 8)
        if n < 64:
            g, j = divmod(n, 8)
            out[n // EACH, rows, :] = image[g * 8 : g * 8 + 8, j * TILE : (j + 1) * TILE]
        elif n < 72 and gram is not None:
            g = n - 64
            out[n // EACH, rows, :] = gram[g * 8 : g * 8 + 8, :]
        else:
            out[n // EACH, rows, :] = jnp.zeros((8, TILE), f32)


def read_packed(packed, n):
    return packed[n // EACH, pl.ds((n % EACH) * 8, 8), :]


def two_parts(x):
    high = x.astype(bf16)
    low = (x - high.astype(f32)).astype(bf16)
    return jnp.concatenate([high, low], axis=0)


def gram_of(parts):
    four = dot_rows(parts, parts)
    two = four[:K] + four[K:]
    return two[:, :K] + two[:, K:]


def reciprocal(x):
    near = pl.reciprocal(x, approx=True)
    near = near * (2.0 - x * near)
    return near * (2.0 - x * near)


def inverse_factor(gram):
    shape = (K, 2 * K)
    row = lax.broadcasted_iota(jnp.int32, shape, 0)
    col = lax.broadcasted_iota(jnp.int32, shape, 1)
    rest = jnp.concatenate([gram, (row[:, :K] == col[:, :K]).astype(f32)], axis=1)
    finished = []
    for k in range(0, K, PANEL):
        here = (K - k, 2 * K)
        below = row[: K - k]
        columns = [jnp.broadcast_to(rest[:, k + j : k + j + 1], here) for j in range(PANEL)]
        lines = [rest[j : j + 1, :] for j in range(PANEL)]
        for j in range(PANEL):
            inverse = reciprocal(columns[j][j : j + 1, :])
            factor = jnp.where(below > j, columns[j] * inverse, 0.0)
            for later in range(j + 1, PANEL):
                columns[later] = columns[later] - factor * columns[later][j : j + 1, :]
                lines[later] = lines[later] - factor[later : later + 1, :] * lines[j]
            rest = rest - factor * lines[j]
        finished.append(rest[:PANEL])
        rest = rest[PANEL:]
    work = jnp.concatenate(finished, axis=0)
    diagonal = jnp.sum(jnp.where(row == col, work, 0.0), axis=1, keepdims=True)
    return work[:, K:] * lax.rsqrt(diagonal)


def start_kernel(row_blocks, col_blocks, live, turn, tiles, basis, dense, packed, stock, first, sems, first_sem):
    get_basis = pltpu.make_async_copy(basis, first, first_sem)
    get_basis.start()
    copies = []
    for n in range(BATCHES):
        span = pl.ds(n * BATCH, BATCH)
        copies.append(pltpu.make_async_copy(tiles.at[span], stock.at[span], sems.at[n]))
        copies[-1].start()
    core, count = turn[0], live[0]

    def window(s):
        col = col_blocks[s]
        quarter = col // (CB // 4)
        position = (((quarter % 2) ^ core) * 2 + quarter // 2) * (CB // 4) + col % (CB // 4)
        return (
            pl.ds(pl.multiple_of(row_blocks[s] * TILE, TILE), TILE),
            pl.ds(pl.multiple_of(position * TILE, TILE), TILE),
        )

    def put(s, carry):
        dense[window(s)] = jnp.where(s < count, stock[s], jnp.zeros((TILE, TILE), bf16))
        return carry

    for n in range(BATCHES):
        copies[n].wait()
        lax.fori_loop(n * BATCH, (n + 1) * BATCH, put, 0, unroll=8)
    get_basis.wait()
    image = jnp.zeros((K, HEIGHT), f32)
    for p in range(4):
        q = (p % 2) * 2 + ((p // 2) ^ core)
        part = first[:, pl.ds(pl.multiple_of(q * OWN, OWN), OWN)]
        image = image + dot_rows(part, dense[:, p * OWN : (p + 1) * OWN])
    write_packed(packed, image, None)


def gathered(chunk, mine, other, dense):
    image, grams = 0.0, []
    for p, half in ((chunk, mine), (2 + chunk, other)):
        parts = two_parts(half[...])
        grams.append(gram_of(parts))
        image = image + dot_rows(parts, dense[:, p * OWN : (p + 1) * OWN])
    return image[:K] + image[K:], grams[0] + grams[1]


def forward_kernel(mine, other, dense, image, gram):
    image[...], gram[...] = gathered(0, mine, other, dense)


def forward_last_kernel(mine, other, dense, image_before, gram_before, packed):
    image, gram = gathered(1, mine, other, dense)
    gram = gram_before[...] + gram
    write_packed(packed, image_before[...] + image, jnp.concatenate([gram, gram], axis=1))


def gram_kernel(own, out):
    gram = gram_of(two_parts(own[...]))
    out[...] = jnp.concatenate([gram[: K // 2], gram[K // 2 :]], axis=1)


def image_of(packed):
    return jnp.concatenate(
        [jnp.concatenate([read_packed(packed, g * 8 + j) for j in range(8)], axis=1) for g in range(8)],
        axis=0,
    )


def spread(chunk, image_half, dense, mine, other):
    for p, target in ((chunk, mine), (2 + chunk, other)):
        for n in range(2):
            width = OWN // 2
            source = pl.ds(p * OWN + n * width, width)
            product = jnp.dot(image_half, dense[:, source], preferred_element_type=f32)
            target[:, n * width : (n + 1) * width] = product


def first_backward_kernel(packed, dense, mine, other, kept):
    kept[...] = image_of(packed).astype(bf16)
    spread(0, kept[...], dense, mine, other)


def backward_kernel(packed, dense, mine, other, kept, inverse):
    gram = jnp.concatenate([read_packed(packed, 64 + g) for g in range(8)], axis=0)[:, :K]
    found = inverse_factor(gram * (1.0 / CELLS))
    inverse[...] = found
    image = jnp.dot(found, image_of(packed), precision=lax.Precision.HIGHEST, preferred_element_type=f32)
    kept[...] = image.astype(bf16)
    spread(0, kept[...], dense, mine, other)


def backward_last_kernel(kept, dense, mine, other):
    spread(1, kept[...], dense, mine, other)


def add_kernel(a, b, out):
    out[...] = a[...] + b[...]


def share_kernel(parts, out):
    total = parts[0]
    for n in range(1, parts.shape[0]):
        total = total + parts[n]
    for n in range(out.shape[0]):
        out[n] = total


def finish_kernel(turn, gram, *refs):
    halves, last_half, inverses, out = refs[: 2 * ITERS - 2], refs[2 * ITERS - 2], refs[2 * ITERS - 1 : -1], refs[-1]
    whole = jnp.concatenate([gram[:, :K], gram[:, K:]], axis=0)
    last = inverse_factor(whole * (1.0 / CELLS))
    for i in range(ITERS):
        if i < ITERS - 1:
            found, taken = inverses[i][...], jnp.where(turn[1] == 0, halves[2 * i][...], halves[2 * i + 1][...])
        else:
            found, taken = last, last_half[...]
        out[i] = jnp.dot(found, taken, precision=lax.Precision.HIGHEST, preferred_element_type=f32)


def shifted(x, axis, by):
    count = lax.axis_size(axis)
    return lax.ppermute(x, axis, [(i, (i + by) % count) for i in range(count)])


def summed_by_all(x, axes):
    count = lax.axis_size(axes)
    return jnp.sum(lax.all_to_all(jnp.broadcast_to(x[None], (count, *x.shape)), axes, 0, 0, tiled=True), axis=0)


def call(kernel, name, mib, ins, outs, arrays, flops=0, scratch=()):
    shapes = tuple(jax.ShapeDtypeStruct(*o) for o in outs)
    moved = sum(a.size * a.dtype.itemsize for a in (*arrays, *shapes))
    found = pl.pallas_call(
        kernel,
        out_shape=shapes,
        in_specs=ins,
        out_specs=(VMEM,) * len(outs),
        scratch_shapes=list(scratch),
        compiler_params=params(mib),
        cost_estimate=pl.CostEstimate(flops=flops, bytes_accessed=moved, transcendentals=0),
        name=name,
    )(*arrays)
    return found[0] if len(outs) == 1 else found


def shared(parts, count):
    return call(share_kernel, "share", 4, [VMEM], [((count, *parts.shape[1:]), f32)], [parts])


def added(a, b):
    return call(add_kernel, "add", 4, [VMEM, VMEM], [(a.shape, f32)], [a, b])


def summed_over_blk(packed):
    shares = lax.all_to_all(packed, PLANE, 0, 0, tiled=True)
    shares = lax.all_to_all(shared(shares, 4), "h", 0, 0, tiled=True)
    return lax.all_to_all(shared(shares, PEERS), PLANE, 0, 0, tiled=True)


def local(sens_tiles, start_basis, row_blocks, col_blocks, live_counts):
    core, low = lax.axis_index("c"), lax.axis_index("l")
    turn = jnp.stack([core, low]).astype(jnp.int32)
    packed_shape = ((PEERS, EACH * 8, TILE), f32)
    chunk, square, kept_shape = ((K, OWN), f32), ((K, K), f32), ((K, HEIGHT), bf16)
    work = 2 * K * HEIGHT * HALF
    dense, packed = call(
        start_kernel,
        "start",
        START_MIB,
        [SMEM, SMEM, SMEM, SMEM, HBM, HBM],
        [((HEIGHT, WIDTH), bf16), packed_shape],
        [row_blocks.reshape(MAXB), col_blocks.reshape(MAXB), live_counts.reshape(1), turn, sens_tiles, start_basis],
        2 * work,
        [
            pltpu.VMEM(sens_tiles.shape, bf16),
            pltpu.VMEM(start_basis.shape, bf16),
            pltpu.SemaphoreType.DMA((BATCHES,)),
            pltpu.SemaphoreType.DMA,
        ],
    )
    halves, inverses = [], []
    for iteration in range(ITERS):
        packed = summed_over_blk(packed)
        if iteration == 0:
            mine, other, kept = call(first_backward_kernel, "backward", 8, [VMEM, VMEM], [chunk, chunk, kept_shape], [packed, dense], work)
        else:
            mine, other, kept, inverse = call(
                backward_kernel, "backward", 8, [VMEM, VMEM], [chunk, chunk, kept_shape, square], [packed, dense], work
            )
            inverses.append(inverse)
        moving = shifted(other, "c", 1)
        mine_last, other_last = call(backward_last_kernel, "backward_last", 8, [VMEM, VMEM], [chunk, chunk], [kept, dense], work)
        mine = added(mine, moving)
        if iteration == ITERS - 1:
            mine_last = added(mine_last, shifted(other_last, "c", 1))
            own = jnp.where(low == 0, mine, mine_last)
            sent = jnp.where(low == 0, mine_last, mine)
            own = own + shifted(sent, "l", 1)
            break
        moving = shifted(mine, "l", 1)
        mine_last = added(mine_last, shifted(other_last, "c", 1))
        moving_last = shifted(mine_last, "l", 1)
        mine, mine_last = lax.optimization_barrier((mine, mine_last))
        mine = added(mine, moving)
        image, gram = call(
            forward_kernel, "forward", 12, [VMEM, VMEM, VMEM], [chunk, square], [mine, shifted(mine, "c", 1), dense], 2 * work
        )
        mine_last = added(mine_last, moving_last)
        packed = call(
            forward_last_kernel,
            "forward_last",
            12,
            [VMEM] * 5,
            [packed_shape],
            [mine_last, shifted(mine_last, "c", 1), dense, image, gram],
            2 * work,
        )
        halves += [mine, mine_last]
    gram = call(gram_kernel, "gram", 50, [VMEM], [((K // 2, 2 * K), f32)], [own])
    gram = summed_by_all(summed_by_all(gram + shifted(gram, "c", 1), PLANE), ("h", "l"))
    return call(
        finish_kernel,
        "finish",
        50,
        [SMEM] + [VMEM] * (3 * ITERS - 1),
        [((ITERS, K, OWN), f32)],
        [turn, gram, *halves, own, *inverses],
    )


def solution(mesh):
    fine = Mesh(mesh.devices.reshape(4, 4, 4, 2, 2), BLK + ROWS)
    in_specs = (
        P(BLK, ROWS, None),
        P(None, BLK),
        P(BLK, ROWS),
        P(BLK, ROWS),
        P(BLK, ROWS),
    )
    out_specs = P(None, None, BLK + ROWS)
    return jax.shard_map(local, mesh=fine, in_specs=in_specs, out_specs=out_specs, check_vma=False)
```

```python
import jax
import jax.numpy as jnp
from jax import lax
from jax.experimental import pallas as pl
from jax.experimental.pallas import tpu as pltpu
from jax.sharding import Mesh
from jax.sharding import PartitionSpec as P

TILE = 128
K = 64
RB = 8
CB = 32
MAXB = 256
ITERS = 4
CELLS = 262144.0
WIDTH = CB * TILE
HEIGHT = RB * TILE
HALF = WIDTH // 2
OWN = WIDTH // 4
PEERS = 16
EACH = 5
LIVE, CORE, LOW = 2 * MAXB, 2 * MAXB + 1, 2 * MAXB + 2
PANEL = 8
START_MIB = 40
BATCHES = 8
BATCH = MAXB // BATCHES

f32 = jnp.float32
bf16 = jnp.bfloat16
BLK = ("y", "x", "h")
ROWS = ("l", "c")
PLANE = ("y", "x")
VMEM = pl.BlockSpec(memory_space=pltpu.VMEM)
SMEM = pl.BlockSpec(memory_space=pltpu.SMEM)
HBM = pl.BlockSpec(memory_space=pltpu.HBM)


def dot_rows(a, b):
    return lax.dot_general(a, b, (((1,), (1,)), ((), ())), preferred_element_type=f32)


def params(mib):
    return pltpu.CompilerParams(vmem_limit_bytes=mib << 20)


def write_packed(out, image, gram):
    for n in range(PEERS * EACH):
        rows = pl.ds((n % EACH) * 8, 8)
        if n < 64:
            g, j = divmod(n, 8)
            out[n // EACH, rows, :] = image[g * 8 : g * 8 + 8, j * TILE : (j + 1) * TILE]
        elif n < 72 and gram is not None:
            g = n - 64
            out[n // EACH, rows, :] = gram[g * 8 : g * 8 + 8, :]
        else:
            out[n // EACH, rows, :] = jnp.zeros((8, TILE), f32)


def read_packed(packed, n):
    return packed[n // EACH, pl.ds((n % EACH) * 8, 8), :]


def two_parts(x):
    high = x.astype(bf16)
    low = (x - high.astype(f32)).astype(bf16)
    return jnp.concatenate([high, low], axis=0)


def gram_of(parts):
    four = dot_rows(parts, parts)
    two = four[:K] + four[K:]
    return two[:, :K] + two[:, K:]


def reciprocal(x):
    near = pl.reciprocal(x, approx=True)
    near = near * (2.0 - x * near)
    return near * (2.0 - x * near)


def inverse_factor(gram):
    shape = (K, 2 * K)
    row = lax.broadcasted_iota(jnp.int32, shape, 0)
    col = lax.broadcasted_iota(jnp.int32, shape, 1)
    rest = jnp.concatenate([gram, (row[:, :K] == col[:, :K]).astype(f32)], axis=1)
    finished = []
    for k in range(0, K, PANEL):
        here = (K - k, 2 * K)
        below = row[: K - k]
        columns = [jnp.broadcast_to(rest[:, k + j : k + j + 1], here) for j in range(PANEL)]
        lines = [rest[j : j + 1, :] for j in range(PANEL)]
        for j in range(PANEL):
            inverse = reciprocal(columns[j][j : j + 1, :])
            factor = jnp.where(below > j, columns[j] * inverse, 0.0)
            for later in range(j + 1, PANEL):
                columns[later] = columns[later] - factor * columns[later][j : j + 1, :]
                lines[later] = lines[later] - factor[later : later + 1, :] * lines[j]
            rest = rest - factor * lines[j]
        finished.append(rest[:PANEL])
        rest = rest[PANEL:]
    work = jnp.concatenate(finished, axis=0)
    diagonal = jnp.sum(jnp.where(row == col, work, 0.0), axis=1, keepdims=True)
    return work[:, K:] * lax.rsqrt(diagonal)


def start_kernel(numbers, tiles, basis, dense, packed, stock, first, sems, first_sem):
    get_basis = pltpu.make_async_copy(basis, first, first_sem)
    get_basis.start()
    copies = []
    for n in range(BATCHES):
        span = pl.ds(n * BATCH, BATCH)
        copies.append(pltpu.make_async_copy(tiles.at[span], stock.at[span], sems.at[n]))
        copies[-1].start()
    core, count = numbers[CORE], numbers[LIVE]

    def window(s):
        col = numbers[MAXB + s]
        quarter = col // (CB // 4)
        position = (((quarter % 2) ^ core) * 2 + quarter // 2) * (CB // 4) + col % (CB // 4)
        return (
            pl.ds(pl.multiple_of(numbers[s] * TILE, TILE), TILE),
            pl.ds(pl.multiple_of(position * TILE, TILE), TILE),
        )

    def put(s, carry):
        dense[window(s)] = jnp.where(s < count, stock[s], jnp.zeros((TILE, TILE), bf16))
        return carry

    for n in range(BATCHES):
        copies[n].wait()
        lax.fori_loop(n * BATCH, (n + 1) * BATCH, put, 0, unroll=8)
    get_basis.wait()
    image = jnp.zeros((K, HEIGHT), f32)
    for p in range(4):
        q = (p % 2) * 2 + ((p // 2) ^ core)
        part = first[:, pl.ds(pl.multiple_of(q * OWN, OWN), OWN)]
        image = image + dot_rows(part, dense[:, p * OWN : (p + 1) * OWN])
    write_packed(packed, image, None)


def gathered(chunk, mine, other, dense):
    image, grams = 0.0, []
    for p, half in ((chunk, mine), (2 + chunk, other)):
        parts = two_parts(half[...])
        grams.append(gram_of(parts))
        image = image + dot_rows(parts, dense[:, p * OWN : (p + 1) * OWN])
    return image[:K] + image[K:], grams[0] + grams[1]


def forward_kernel(mine, upper, lower, dense, image, gram):
    other = jnp.concatenate([upper[...], lower[...]], axis=0)
    image[...], gram[...] = gathered(0, mine, other, dense)


def forward_last_kernel(mine, other, dense, image_before, gram_before, packed):
    image, gram = gathered(1, mine, other, dense)
    gram = gram_before[...] + gram
    write_packed(packed, image_before[...] + image, jnp.concatenate([gram, gram], axis=1))


def gram_kernel(own, out):
    gram = gram_of(two_parts(own[...]))
    out[...] = jnp.concatenate([gram[: K // 2], gram[K // 2 :]], axis=1)


def image_of(packed):
    return jnp.concatenate(
        [jnp.concatenate([read_packed(packed, g * 8 + j) for j in range(8)], axis=1) for g in range(8)],
        axis=0,
    )


def spread(chunk, image_half, dense, mine, other):
    for p, target in ((chunk, mine), (2 + chunk, other)):
        for n in range(2):
            width = OWN // 2
            source = pl.ds(p * OWN + n * width, width)
            product = jnp.dot(image_half, dense[:, source], preferred_element_type=f32)
            target[:, n * width : (n + 1) * width] = product


def first_backward_kernel(packed, dense, mine, other, kept):
    kept[...] = image_of(packed).astype(bf16)
    spread(0, kept[...], dense, mine, other)


def backward_kernel(packed, dense, mine, other, kept, inverse):
    gram = jnp.concatenate([read_packed(packed, 64 + g) for g in range(8)], axis=0)[:, :K]
    found = inverse_factor(gram * (1.0 / CELLS))
    inverse[...] = found
    image = jnp.dot(found, image_of(packed), precision=lax.Precision.HIGHEST, preferred_element_type=f32)
    kept[...] = image.astype(bf16)
    spread(0, kept[...], dense, mine, other)


def backward_last_kernel(kept, dense, mine, other):
    spread(1, kept[...], dense, mine, other)


def add_kernel(a, b, out):
    out[...] = a[...] + b[...]


def add_parts_kernel(a, b, out, upper, lower):
    total = a[...] + b[...]
    out[...] = total
    upper[...] = total[: K // 2]
    lower[...] = total[K // 2 :]


def share_kernel(parts, out):
    total = parts[0]
    for n in range(1, parts.shape[0]):
        total = total + parts[n]
    for n in range(out.shape[0]):
        out[n] = total


def settle_kernel(numbers, inverse, half, half_last, out):
    taken = jnp.where(numbers[LOW] == 0, half[...], half_last[...])
    out[...] = jnp.dot(inverse[...], taken, precision=lax.Precision.HIGHEST, preferred_element_type=f32)


def finish_kernel(gram, own, *refs):
    settled, out = refs[:-1], refs[-1]
    whole = jnp.concatenate([gram[:, :K], gram[:, K:]], axis=0)
    last = inverse_factor(whole * (1.0 / CELLS))
    for i, ready in enumerate(settled):
        out[i] = ready[...]
    out[ITERS - 1] = jnp.dot(last, own[...], precision=lax.Precision.HIGHEST, preferred_element_type=f32)


def shifted(x, axis, by):
    count = lax.axis_size(axis)
    return lax.ppermute(x, axis, [(i, (i + by) % count) for i in range(count)])


def summed_by_all(x, axes):
    count = lax.axis_size(axes)
    return jnp.sum(lax.all_to_all(jnp.broadcast_to(x[None], (count, *x.shape)), axes, 0, 0, tiled=True), axis=0)


def call(kernel, name, mib, ins, outs, arrays, flops=0, scratch=()):
    shapes = tuple(jax.ShapeDtypeStruct(*o) for o in outs)
    moved = sum(a.size * a.dtype.itemsize for a in (*arrays, *shapes))
    found = pl.pallas_call(
        kernel,
        out_shape=shapes,
        in_specs=ins,
        out_specs=(VMEM,) * len(outs),
        scratch_shapes=list(scratch),
        compiler_params=params(mib),
        cost_estimate=pl.CostEstimate(flops=flops, bytes_accessed=moved, transcendentals=0),
        name=name,
    )(*arrays)
    return found[0] if len(outs) == 1 else found


def shared(parts, count):
    return call(share_kernel, "share", 4, [VMEM], [((count, *parts.shape[1:]), f32)], [parts])


def added(a, b):
    return call(add_kernel, "add", 4, [VMEM, VMEM], [(a.shape, f32)], [a, b])


def summed_over_blk(packed):
    shares = lax.all_to_all(packed, PLANE, 0, 0, tiled=True)
    shares = lax.all_to_all(shared(shares, 4), "h", 0, 0, tiled=True)
    return lax.all_to_all(shared(shares, PEERS), PLANE, 0, 0, tiled=True)


def local(sens_tiles, start_basis, row_blocks, col_blocks, live_counts):
    core, low = lax.axis_index("c"), lax.axis_index("l")
    places = [row_blocks.reshape(MAXB), col_blocks.reshape(MAXB), live_counts.reshape(1), core.reshape(1), low.reshape(1)]
    numbers = jnp.concatenate([p.astype(jnp.int32) for p in places])
    packed_shape = ((PEERS, EACH * 8, TILE), f32)
    chunk, square, kept_shape = ((K, OWN), f32), ((K, K), f32), ((K, HEIGHT), bf16)
    work = 2 * K * HEIGHT * HALF
    dense, packed = call(
        start_kernel,
        "start",
        START_MIB,
        [SMEM, HBM, HBM],
        [((HEIGHT, WIDTH), bf16), packed_shape],
        [numbers, sens_tiles, start_basis],
        2 * work,
        [
            pltpu.VMEM(sens_tiles.shape, bf16),
            pltpu.VMEM(start_basis.shape, bf16),
            pltpu.SemaphoreType.DMA((BATCHES,)),
            pltpu.SemaphoreType.DMA,
        ],
    )
    halves, settled = None, []
    for iteration in range(ITERS):
        packed = summed_over_blk(packed)
        if iteration == 0:
            mine, other, kept = call(first_backward_kernel, "backward", 8, [VMEM, VMEM], [chunk, chunk, kept_shape], [packed, dense], work)
        else:
            mine, other, kept, inverse = call(
                backward_kernel, "backward", 8, [VMEM, VMEM], [chunk, chunk, kept_shape, square], [packed, dense], work
            )
            settled.append(
                call(settle_kernel, "settle", 4, [SMEM] + [VMEM] * 3, [chunk], [numbers, inverse, *halves], 6 * 2 * K * K * OWN)
            )
        moving = shifted(other, "c", 1)
        mine_last, other_last = call(backward_last_kernel, "backward_last", 8, [VMEM, VMEM], [chunk, chunk], [kept, dense], work)
        mine = added(mine, moving)
        if iteration == ITERS - 1:
            mine_last = added(mine_last, shifted(other_last, "c", 1))
            own = jnp.where(low == 0, mine, mine_last)
            sent = jnp.where(low == 0, mine_last, mine)
            own = own + shifted(sent, "l", 1)
            break
        moving = shifted(mine, "l", 1)
        mine_last = added(mine_last, shifted(other_last, "c", 1))
        moving_last = shifted(mine_last, "l", 1)
        mine, mine_last = lax.optimization_barrier((mine, mine_last))
        part = ((K // 2, OWN), f32)
        mine, upper, lower = call(add_parts_kernel, "add_parts", 4, [VMEM, VMEM], [chunk, part, part], [mine, moving])
        image, gram = call(
            forward_kernel,
            "forward",
            12,
            [VMEM] * 4,
            [chunk, square],
            [mine, shifted(upper, "c", 1), shifted(lower, "c", 1), dense],
            2 * work,
        )
        mine_last, image, gram = lax.optimization_barrier((mine_last, image, gram))
        mine_last = added(mine_last, moving_last)
        packed = call(
            forward_last_kernel,
            "forward_last",
            12,
            [VMEM] * 5,
            [packed_shape],
            [mine_last, shifted(mine_last, "c", 1), dense, image, gram],
            2 * work,
        )
        halves = mine, mine_last
    gram = call(gram_kernel, "gram", 50, [VMEM], [((K // 2, 2 * K), f32)], [own])
    gram = summed_by_all(summed_by_all(gram + shifted(gram, "c", 1), PLANE), ("h", "l"))
    return call(
        finish_kernel, "finish", 50, [VMEM] * (ITERS + 1), [((ITERS, K, OWN), f32)], [gram, own, *settled]
    )


def solution(mesh):
    fine = Mesh(mesh.devices.reshape(4, 4, 4, 2, 2), BLK + ROWS)
    in_specs = (
        P(BLK, ROWS, None),
        P(None, BLK),
        P(BLK, ROWS),
        P(BLK, ROWS),
        P(BLK, ROWS),
    )
    out_specs = P(None, None, BLK + ROWS)
    return jax.shard_map(local, mesh=fine, in_specs=in_specs, out_specs=out_specs, check_vma=False)
```

```python
import jax
import jax.numpy as jnp
from jax import lax
from jax.experimental import pallas as pl
from jax.experimental.pallas import tpu as pltpu
from jax.sharding import Mesh
from jax.sharding import PartitionSpec as P

TILE = 128
K = 64
RB = 8
CB = 32
MAXB = 256
ITERS = 4
CELLS = 262144.0
WIDTH = CB * TILE
HEIGHT = RB * TILE
HALF = WIDTH // 2
OWN = WIDTH // 4
PEERS = 16
EACH = 5
LIVE, CORE, LOW = 2 * MAXB, 2 * MAXB + 1, 2 * MAXB + 2
PANEL = 8
START_MIB = 40
BATCHES = 8
BATCH = MAXB // BATCHES

f32 = jnp.float32
bf16 = jnp.bfloat16
BLK = ("y", "x", "h")
ROWS = ("l", "c")
PLANE = ("y", "x")
VMEM = pl.BlockSpec(memory_space=pltpu.VMEM)
SMEM = pl.BlockSpec(memory_space=pltpu.SMEM)
HBM = pl.BlockSpec(memory_space=pltpu.HBM)


def dot_rows(a, b):
    return lax.dot_general(a, b, (((1,), (1,)), ((), ())), preferred_element_type=f32)


def params(mib):
    return pltpu.CompilerParams(vmem_limit_bytes=mib << 20)


def write_packed(out, image, gram):
    for n in range(PEERS * EACH):
        rows = pl.ds((n % EACH) * 8, 8)
        if n < 64:
            g, j = divmod(n, 8)
            out[n // EACH, rows, :] = image[g * 8 : g * 8 + 8, j * TILE : (j + 1) * TILE]
        elif n < 72 and gram is not None:
            g = n - 64
            out[n // EACH, rows, :] = gram[g * 8 : g * 8 + 8, :]
        else:
            out[n // EACH, rows, :] = jnp.zeros((8, TILE), f32)


def read_packed(packed, n):
    return packed[n // EACH, pl.ds((n % EACH) * 8, 8), :]


def two_parts(x):
    high = x.astype(bf16)
    low = (x - high.astype(f32)).astype(bf16)
    return jnp.concatenate([high, low], axis=0)


def gram_of(parts):
    four = dot_rows(parts, parts)
    two = four[:K] + four[K:]
    return two[:, :K] + two[:, K:]


def reciprocal(x):
    near = pl.reciprocal(x, approx=True)
    near = near * (2.0 - x * near)
    return near * (2.0 - x * near)


def inverse_factor(gram):
    shape = (K, 2 * K)
    row = lax.broadcasted_iota(jnp.int32, shape, 0)
    col = lax.broadcasted_iota(jnp.int32, shape, 1)
    rest = jnp.concatenate([gram, (row[:, :K] == col[:, :K]).astype(f32)], axis=1)
    finished = []
    for k in range(0, K, PANEL):
        here = (K - k, 2 * K)
        below = row[: K - k]
        columns = [jnp.broadcast_to(rest[:, k + j : k + j + 1], here) for j in range(PANEL)]
        lines = [rest[j : j + 1, :] for j in range(PANEL)]
        for j in range(PANEL):
            inverse = reciprocal(columns[j][j : j + 1, :])
            factor = jnp.where(below > j, columns[j] * inverse, 0.0)
            for later in range(j + 1, PANEL):
                columns[later] = columns[later] - factor * columns[later][j : j + 1, :]
                lines[later] = lines[later] - factor[later : later + 1, :] * lines[j]
            rest = rest - factor * lines[j]
        finished.append(rest[:PANEL])
        rest = rest[PANEL:]
    work = jnp.concatenate(finished, axis=0)
    diagonal = jnp.sum(jnp.where(row == col, work, 0.0), axis=1, keepdims=True)
    return work[:, K:] * lax.rsqrt(diagonal)


def start_kernel(numbers, tiles, basis, dense, packed, stock, first, sems, first_sem):
    get_basis = pltpu.make_async_copy(basis, first, first_sem)
    get_basis.start()
    copies = []
    for n in range(BATCHES):
        span = pl.ds(n * BATCH, BATCH)
        copies.append(pltpu.make_async_copy(tiles.at[span], stock.at[span], sems.at[n]))
        copies[-1].start()
    core, count = numbers[CORE], numbers[LIVE]

    def window(s):
        col = numbers[MAXB + s]
        quarter = col // (CB // 4)
        position = (((quarter % 2) ^ core) * 2 + quarter // 2) * (CB // 4) + col % (CB // 4)
        return (
            pl.ds(pl.multiple_of(numbers[s] * TILE, TILE), TILE),
            pl.ds(pl.multiple_of(position * TILE, TILE), TILE),
        )

    def put(s, carry):
        dense[window(s)] = jnp.where(s < count, stock[s], jnp.zeros((TILE, TILE), bf16))
        return carry

    for n in range(BATCHES):
        copies[n].wait()
        lax.fori_loop(n * BATCH, (n + 1) * BATCH, put, 0, unroll=8)
    get_basis.wait()
    image = jnp.zeros((K, HEIGHT), f32)
    for p in range(4):
        q = (p % 2) * 2 + ((p // 2) ^ core)
        part = first[:, pl.ds(pl.multiple_of(q * OWN, OWN), OWN)]
        image = image + dot_rows(part, dense[:, p * OWN : (p + 1) * OWN])
    write_packed(packed, image, None)


def gathered(p, half, dense):
    parts = two_parts(half)
    image = dot_rows(parts, dense[:, p * OWN : (p + 1) * OWN])
    return image[:K] + image[K:], gram_of(parts)


def forward_kernel(mine, upper, lower, dense, image, gram):
    image_mine, gram_mine = gathered(0, mine[...], dense)
    image_other, gram_other = gathered(2, jnp.concatenate([upper[...], lower[...]], axis=0), dense)
    image[...] = image_mine + image_other
    gram[...] = gram_mine + gram_other


def forward_mine_kernel(mine, dense, image_before, image, gram):
    found, gram[...] = gathered(1, mine[...], dense)
    image[...] = image_before[...] + found


def forward_last_kernel(other, dense, image_before, gram_before, gram_mine, packed):
    found, gram_other = gathered(3, other[...], dense)
    gram = gram_before[...] + (gram_mine[...] + gram_other)
    write_packed(packed, image_before[...] + found, jnp.concatenate([gram, gram], axis=1))


def gram_kernel(own, out):
    gram = gram_of(two_parts(own[...]))
    out[...] = jnp.concatenate([gram[: K // 2], gram[K // 2 :]], axis=1)


def image_of(packed):
    return jnp.concatenate(
        [jnp.concatenate([read_packed(packed, g * 8 + j) for j in range(8)], axis=1) for g in range(8)],
        axis=0,
    )


def spread(chunk, image_half, dense, mine, other):
    for p, target in ((chunk, mine), (2 + chunk, other)):
        for n in range(2):
            width = OWN // 2
            source = pl.ds(p * OWN + n * width, width)
            product = jnp.dot(image_half, dense[:, source], preferred_element_type=f32)
            target[:, n * width : (n + 1) * width] = product


def first_backward_kernel(packed, dense, mine, other, kept):
    kept[...] = image_of(packed).astype(bf16)
    spread(0, kept[...], dense, mine, other)


def backward_kernel(packed, dense, mine, other, kept, inverse):
    gram = jnp.concatenate([read_packed(packed, 64 + g) for g in range(8)], axis=0)[:, :K]
    found = inverse_factor(gram * (1.0 / CELLS))
    inverse[...] = found
    image = jnp.dot(found, image_of(packed), precision=lax.Precision.HIGHEST, preferred_element_type=f32)
    kept[...] = image.astype(bf16)
    spread(0, kept[...], dense, mine, other)


def backward_last_kernel(kept, dense, mine, other):
    spread(1, kept[...], dense, mine, other)


def add_kernel(a, b, out):
    out[...] = a[...] + b[...]


def add_parts_kernel(a, b, out, upper, lower):
    total = a[...] + b[...]
    out[...] = total
    upper[...] = total[: K // 2]
    lower[...] = total[K // 2 :]


def share_kernel(parts, out):
    total = parts[0]
    for n in range(1, parts.shape[0]):
        total = total + parts[n]
    for n in range(out.shape[0]):
        out[n] = total


def settle_kernel(numbers, inverse, half, half_last, out):
    taken = jnp.where(numbers[LOW] == 0, half[...], half_last[...])
    out[...] = jnp.dot(inverse[...], taken, precision=lax.Precision.HIGHEST, preferred_element_type=f32)


def finish_kernel(gram, own, *refs):
    settled, out = refs[:-1], refs[-1]
    whole = jnp.concatenate([gram[:, :K], gram[:, K:]], axis=0)
    last = inverse_factor(whole * (1.0 / CELLS))
    for i, ready in enumerate(settled):
        out[i] = ready[...]
    out[ITERS - 1] = jnp.dot(last, own[...], precision=lax.Precision.HIGHEST, preferred_element_type=f32)


def shifted(x, axis, by):
    count = lax.axis_size(axis)
    return lax.ppermute(x, axis, [(i, (i + by) % count) for i in range(count)])


def summed_by_all(x, axes):
    count = lax.axis_size(axes)
    return jnp.sum(lax.all_to_all(jnp.broadcast_to(x[None], (count, *x.shape)), axes, 0, 0, tiled=True), axis=0)


def call(kernel, name, mib, ins, outs, arrays, flops=0, scratch=()):
    shapes = tuple(jax.ShapeDtypeStruct(*o) for o in outs)
    moved = sum(a.size * a.dtype.itemsize for a in (*arrays, *shapes))
    found = pl.pallas_call(
        kernel,
        out_shape=shapes,
        in_specs=ins,
        out_specs=(VMEM,) * len(outs),
        scratch_shapes=list(scratch),
        compiler_params=params(mib),
        cost_estimate=pl.CostEstimate(flops=flops, bytes_accessed=moved, transcendentals=0),
        name=name,
    )(*arrays)
    return found[0] if len(outs) == 1 else found


def shared(parts, count):
    return call(share_kernel, "share", 4, [VMEM], [((count, *parts.shape[1:]), f32)], [parts])


def added(a, b):
    return call(add_kernel, "add", 4, [VMEM, VMEM], [(a.shape, f32)], [a, b])


def summed_over_blk(packed):
    shares = lax.all_to_all(packed, PLANE, 0, 0, tiled=True)
    shares = lax.all_to_all(shared(shares, 4), "h", 0, 0, tiled=True)
    return lax.all_to_all(shared(shares, PEERS), PLANE, 0, 0, tiled=True)


def local(sens_tiles, start_basis, row_blocks, col_blocks, live_counts):
    core, low = lax.axis_index("c"), lax.axis_index("l")
    places = [row_blocks.reshape(MAXB), col_blocks.reshape(MAXB), live_counts.reshape(1), core.reshape(1), low.reshape(1)]
    numbers = jnp.concatenate([p.astype(jnp.int32) for p in places])
    packed_shape = ((PEERS, EACH * 8, TILE), f32)
    chunk, square, kept_shape = ((K, OWN), f32), ((K, K), f32), ((K, HEIGHT), bf16)
    work = 2 * K * HEIGHT * HALF
    dense, packed = call(
        start_kernel,
        "start",
        START_MIB,
        [SMEM, HBM, HBM],
        [((HEIGHT, WIDTH), bf16), packed_shape],
        [numbers, sens_tiles, start_basis],
        2 * work,
        [
            pltpu.VMEM(sens_tiles.shape, bf16),
            pltpu.VMEM(start_basis.shape, bf16),
            pltpu.SemaphoreType.DMA((BATCHES,)),
            pltpu.SemaphoreType.DMA,
        ],
    )
    halves, settled = None, []
    for iteration in range(ITERS):
        packed = summed_over_blk(packed)
        if iteration == 0:
            mine, other, kept = call(first_backward_kernel, "backward", 8, [VMEM, VMEM], [chunk, chunk, kept_shape], [packed, dense], work)
        else:
            mine, other, kept, inverse = call(
                backward_kernel, "backward", 8, [VMEM, VMEM], [chunk, chunk, kept_shape, square], [packed, dense], work
            )
            settled.append(
                call(settle_kernel, "settle", 4, [SMEM] + [VMEM] * 3, [chunk], [numbers, inverse, *halves], 6 * 2 * K * K * OWN)
            )
        moving = shifted(other, "c", 1)
        mine_last, other_last = call(backward_last_kernel, "backward_last", 8, [VMEM, VMEM], [chunk, chunk], [kept, dense], work)
        mine = added(mine, moving)
        if iteration == ITERS - 1:
            mine_last = added(mine_last, shifted(other_last, "c", 1))
            own = jnp.where(low == 0, mine, mine_last)
            own, *settled = lax.optimization_barrier((own, *settled))
            sent = jnp.where(low == 0, mine_last, mine)
            own = own + shifted(sent, "l", 1)
            break
        moving = shifted(mine, "l", 1)
        mine_last = added(mine_last, shifted(other_last, "c", 1))
        moving_last = shifted(mine_last, "l", 1)
        mine, mine_last = lax.optimization_barrier((mine, mine_last))
        mine, *settled = lax.optimization_barrier((mine, *settled))
        part = ((K // 2, OWN), f32)
        mine, upper, lower = call(add_parts_kernel, "add_parts", 4, [VMEM, VMEM], [chunk, part, part], [mine, moving])
        image, gram = call(
            forward_kernel,
            "forward",
            12,
            [VMEM] * 4,
            [chunk, square],
            [mine, shifted(upper, "c", 1), shifted(lower, "c", 1), dense],
            2 * work,
        )
        mine_last, image, gram = lax.optimization_barrier((mine_last, image, gram))
        mine_last = added(mine_last, moving_last)
        other_last = shifted(mine_last, "c", 1)
        image, gram_mine = call(
            forward_mine_kernel, "forward_mine", 12, [VMEM] * 3, [chunk, square], [mine_last, dense, image], work
        )
        packed = call(
            forward_last_kernel,
            "forward_last",
            12,
            [VMEM] * 5,
            [packed_shape],
            [other_last, dense, image, gram, gram_mine],
            work,
        )
        halves = mine, mine_last
    gram = call(gram_kernel, "gram", 50, [VMEM], [((K // 2, 2 * K), f32)], [own])
    gram = summed_by_all(summed_by_all(gram + shifted(gram, "c", 1), PLANE), ("h", "l"))
    return call(
        finish_kernel, "finish", 50, [VMEM] * (ITERS + 1), [((ITERS, K, OWN), f32)], [gram, own, *settled]
    )


def solution(mesh):
    fine = Mesh(mesh.devices.reshape(4, 4, 4, 2, 2), BLK + ROWS)
    in_specs = (
        P(BLK, ROWS, None),
        P(None, BLK),
        P(BLK, ROWS),
        P(BLK, ROWS),
        P(BLK, ROWS),
    )
    out_specs = P(None, None, BLK + ROWS)
    return jax.shard_map(local, mesh=fine, in_specs=in_specs, out_specs=out_specs, check_vma=False)
```

```python
import jax
import jax.numpy as jnp
from jax import lax
from jax.experimental import pallas as pl
from jax.experimental.pallas import tpu as pltpu
from jax.sharding import Mesh
from jax.sharding import PartitionSpec as P

TILE = 128
K = 64
RB = 8
CB = 32
MAXB = 256
ITERS = 4
CELLS = 262144.0
WIDTH = CB * TILE
HEIGHT = RB * TILE
HALF = WIDTH // 2
OWN = WIDTH // 4
PEERS = 16
EACH = 5
PANEL = 8
START_MIB = 40
BATCHES = 8
BATCH = MAXB // BATCHES

f32 = jnp.float32
bf16 = jnp.bfloat16
BLK = ("y", "x", "h")
ROWS = ("l", "c")
PLANE = ("y", "x")
VMEM = pl.BlockSpec(memory_space=pltpu.VMEM)
SMEM = pl.BlockSpec(memory_space=pltpu.SMEM)
HBM = pl.BlockSpec(memory_space=pltpu.HBM)


def dot_rows(a, b):
    return lax.dot_general(a, b, (((1,), (1,)), ((), ())), preferred_element_type=f32)


def params(mib):
    return pltpu.CompilerParams(vmem_limit_bytes=mib << 20)


def write_packed(out, image, gram):
    for n in range(PEERS * EACH):
        rows = pl.ds((n % EACH) * 8, 8)
        if n < 64:
            g, j = divmod(n, 8)
            out[n // EACH, rows, :] = image[g * 8 : g * 8 + 8, j * TILE : (j + 1) * TILE]
        elif n < 72 and gram is not None:
            g = n - 64
            out[n // EACH, rows, :] = gram[g * 8 : g * 8 + 8, :]
        else:
            out[n // EACH, rows, :] = jnp.zeros((8, TILE), f32)


def read_packed(packed, n):
    return packed[n // EACH, pl.ds((n % EACH) * 8, 8), :]


def two_parts(x):
    high = x.astype(bf16)
    low = (x - high.astype(f32)).astype(bf16)
    return jnp.concatenate([high, low], axis=0)


def gram_of(parts):
    four = dot_rows(parts, parts)
    two = four[:K] + four[K:]
    return two[:, :K] + two[:, K:]


def reciprocal(x):
    near = pl.reciprocal(x, approx=True)
    near = near * (2.0 - x * near)
    return near * (2.0 - x * near)


def inverse_factor(gram):
    shape = (K, 2 * K)
    row = lax.broadcasted_iota(jnp.int32, shape, 0)
    col = lax.broadcasted_iota(jnp.int32, shape, 1)
    rest = jnp.concatenate([gram, (row[:, :K] == col[:, :K]).astype(f32)], axis=1)
    finished = []
    for k in range(0, K, PANEL):
        here = (K - k, 2 * K)
        below = row[: K - k]
        columns = [jnp.broadcast_to(rest[:, k + j : k + j + 1], here) for j in range(PANEL)]
        lines = [rest[j : j + 1, :] for j in range(PANEL)]
        for j in range(PANEL):
            inverse = reciprocal(columns[j][j : j + 1, :])
            factor = jnp.where(below > j, columns[j] * inverse, 0.0)
            for later in range(j + 1, PANEL):
                columns[later] = columns[later] - factor * columns[later][j : j + 1, :]
                lines[later] = lines[later] - factor[later : later + 1, :] * lines[j]
            rest = rest - factor * lines[j]
        finished.append(rest[:PANEL])
        rest = rest[PANEL:]
    work = jnp.concatenate(finished, axis=0)
    diagonal = jnp.sum(jnp.where(row == col, work, 0.0), axis=1, keepdims=True)
    return work[:, K:] * lax.rsqrt(diagonal)


def start_kernel(row_blocks, col_blocks, live, turn, tiles, basis, dense, packed, stock, first, sems, first_sem):
    get_basis = pltpu.make_async_copy(basis, first, first_sem)
    get_basis.start()
    copies = []
    for n in range(BATCHES):
        span = pl.ds(n * BATCH, BATCH)
        copies.append(pltpu.make_async_copy(tiles.at[span], stock.at[span], sems.at[n]))
        copies[-1].start()
    core, count = turn[0], live[0]

    def window(s):
        col = col_blocks[s]
        quarter = col // (CB // 4)
        position = (((quarter % 2) ^ core) * 2 + quarter // 2) * (CB // 4) + col % (CB // 4)
        return (
            pl.ds(pl.multiple_of(row_blocks[s] * TILE, TILE), TILE),
            pl.ds(pl.multiple_of(position * TILE, TILE), TILE),
        )

    def put(s, carry):
        dense[window(s)] = jnp.where(s < count, stock[s], jnp.zeros((TILE, TILE), bf16))
        return carry

    for n in range(BATCHES):
        copies[n].wait()
        lax.fori_loop(n * BATCH, (n + 1) * BATCH, put, 0, unroll=8)
    get_basis.wait()
    image = jnp.zeros((K, HEIGHT), f32)
    for p in range(4):
        q = (p % 2) * 2 + ((p // 2) ^ core)
        part = first[:, pl.ds(pl.multiple_of(q * OWN, OWN), OWN)]
        image = image + dot_rows(part, dense[:, p * OWN : (p + 1) * OWN])
    write_packed(packed, image, None)


def gathered(p, half, dense):
    parts = two_parts(half)
    image = dot_rows(parts, dense[:, p * OWN : (p + 1) * OWN])
    return image[:K] + image[K:], gram_of(parts)


def forward_kernel(mine, upper, lower, dense, image, gram):
    image_mine, gram_mine = gathered(0, mine[...], dense)
    image_other, gram_other = gathered(2, jnp.concatenate([upper[...], lower[...]], axis=0), dense)
    image[...] = image_mine + image_other
    gram[...] = gram_mine + gram_other


def forward_mine_kernel(mine, dense, image_before, image, gram):
    found, gram[...] = gathered(1, mine[...], dense)
    image[...] = image_before[...] + found


def forward_last_kernel(other, dense, image_before, gram_before, gram_mine, packed):
    found, gram_other = gathered(3, other[...], dense)
    gram = gram_before[...] + (gram_mine[...] + gram_other)
    write_packed(packed, image_before[...] + found, jnp.concatenate([gram, gram], axis=1))


def gram_kernel(own, out):
    gram = gram_of(two_parts(own[...]))
    out[...] = jnp.concatenate([gram[: K // 2], gram[K // 2 :]], axis=1)


def image_of(packed):
    return jnp.concatenate(
        [jnp.concatenate([read_packed(packed, g * 8 + j) for j in range(8)], axis=1) for g in range(8)],
        axis=0,
    )


def spread(chunk, image_half, dense, mine, other):
    for p, target in ((chunk, mine), (2 + chunk, other)):
        for n in range(2):
            width = OWN // 2
            source = pl.ds(p * OWN + n * width, width)
            product = jnp.dot(image_half, dense[:, source], preferred_element_type=f32)
            target[:, n * width : (n + 1) * width] = product


def first_backward_kernel(packed, dense, mine, other, kept):
    kept[...] = image_of(packed).astype(bf16)
    spread(0, kept[...], dense, mine, other)


def backward_kernel(packed, dense, mine, other, kept, inverse):
    gram = jnp.concatenate([read_packed(packed, 64 + g) for g in range(8)], axis=0)[:, :K]
    found = inverse_factor(gram * (1.0 / CELLS))
    inverse[...] = found
    image = jnp.dot(found, image_of(packed), precision=lax.Precision.HIGHEST, preferred_element_type=f32)
    kept[...] = image.astype(bf16)
    spread(0, kept[...], dense, mine, other)


def backward_last_kernel(kept, dense, mine, other):
    spread(1, kept[...], dense, mine, other)


def add_kernel(a, b, out):
    out[...] = a[...] + b[...]


def add_parts_kernel(a, b, out, upper, lower):
    total = a[...] + b[...]
    out[...] = total
    upper[...] = total[: K // 2]
    lower[...] = total[K // 2 :]


def share_kernel(parts, out):
    total = parts[0]
    for n in range(1, parts.shape[0]):
        total = total + parts[n]
    for n in range(out.shape[0]):
        out[n] = total


def settle_kernel(turn, inverse, half, half_last, out):
    taken = jnp.where(turn[1] == 0, half[...], half_last[...])
    out[...] = jnp.dot(inverse[...], taken, precision=lax.Precision.HIGHEST, preferred_element_type=f32)


def finish_kernel(gram, own, *refs):
    settled, out = refs[:-1], refs[-1]
    whole = jnp.concatenate([gram[:, :K], gram[:, K:]], axis=0)
    last = inverse_factor(whole * (1.0 / CELLS))
    for i, ready in enumerate(settled):
        out[i] = ready[...]
    out[ITERS - 1] = jnp.dot(last, own[...], precision=lax.Precision.HIGHEST, preferred_element_type=f32)


def shifted(x, axis, by):
    count = lax.axis_size(axis)
    return lax.ppermute(x, axis, [(i, (i + by) % count) for i in range(count)])


def summed_by_all(x, axes):
    count = lax.axis_size(axes)
    return jnp.sum(lax.all_to_all(jnp.broadcast_to(x[None], (count, *x.shape)), axes, 0, 0, tiled=True), axis=0)


def call(kernel, name, mib, ins, outs, arrays, flops=0, scratch=()):
    shapes = tuple(jax.ShapeDtypeStruct(*o) for o in outs)
    moved = sum(a.size * a.dtype.itemsize for a in (*arrays, *shapes))
    found = pl.pallas_call(
        kernel,
        out_shape=shapes,
        in_specs=ins,
        out_specs=(VMEM,) * len(outs),
        scratch_shapes=list(scratch),
        compiler_params=params(mib),
        cost_estimate=pl.CostEstimate(flops=flops, bytes_accessed=moved, transcendentals=0),
        name=name,
    )(*arrays)
    return found[0] if len(outs) == 1 else found


def shared(parts, count):
    return call(share_kernel, "share", 4, [VMEM], [((count, *parts.shape[1:]), f32)], [parts])


def added(a, b):
    return call(add_kernel, "add", 4, [VMEM, VMEM], [(a.shape, f32)], [a, b])


def summed_over_blk(packed):
    shares = lax.all_to_all(packed, PLANE, 0, 0, tiled=True)
    shares = lax.all_to_all(shared(shares, 4), "h", 0, 0, tiled=True)
    return lax.all_to_all(shared(shares, PEERS), PLANE, 0, 0, tiled=True)


def local(sens_tiles, start_basis, row_blocks, col_blocks, live_counts):
    core, low = lax.axis_index("c"), lax.axis_index("l")
    turn = jnp.stack([core, low]).astype(jnp.int32)
    packed_shape = ((PEERS, EACH * 8, TILE), f32)
    chunk, square, kept_shape = ((K, OWN), f32), ((K, K), f32), ((K, HEIGHT), bf16)
    work = 2 * K * HEIGHT * HALF
    dense, packed = call(
        start_kernel,
        "start",
        START_MIB,
        [SMEM, SMEM, SMEM, SMEM, HBM, HBM],
        [((HEIGHT, WIDTH), bf16), packed_shape],
        [row_blocks.reshape(MAXB), col_blocks.reshape(MAXB), live_counts.reshape(1), turn, sens_tiles, start_basis],
        2 * work,
        [
            pltpu.VMEM(sens_tiles.shape, bf16),
            pltpu.VMEM(start_basis.shape, bf16),
            pltpu.SemaphoreType.DMA((BATCHES,)),
            pltpu.SemaphoreType.DMA,
        ],
    )
    halves, settled = None, []
    for iteration in range(ITERS):
        packed = summed_over_blk(packed)
        if iteration == 0:
            mine, other, kept = call(first_backward_kernel, "backward", 8, [VMEM, VMEM], [chunk, chunk, kept_shape], [packed, dense], work)
        else:
            mine, other, kept, inverse = call(
                backward_kernel, "backward", 8, [VMEM, VMEM], [chunk, chunk, kept_shape, square], [packed, dense], work
            )
            settled.append(
                call(settle_kernel, "settle", 4, [SMEM] + [VMEM] * 3, [chunk], [turn, inverse, *halves], 6 * 2 * K * K * OWN)
            )
        moving = shifted(other, "c", 1)
        mine_last, other_last = call(backward_last_kernel, "backward_last", 8, [VMEM, VMEM], [chunk, chunk], [kept, dense], work)
        mine = added(mine, moving)
        if iteration == ITERS - 1:
            mine_last = added(mine_last, shifted(other_last, "c", 1))
            own = jnp.where(low == 0, mine, mine_last)
            own, *settled = lax.optimization_barrier((own, *settled))
            sent = jnp.where(low == 0, mine_last, mine)
            own = own + shifted(sent, "l", 1)
            break
        moving = shifted(mine, "l", 1)
        mine_last = added(mine_last, shifted(other_last, "c", 1))
        moving_last = shifted(mine_last, "l", 1)
        mine, mine_last = lax.optimization_barrier((mine, mine_last))
        mine, *settled = lax.optimization_barrier((mine, *settled))
        part = ((K // 2, OWN), f32)
        mine, upper, lower = call(add_parts_kernel, "add_parts", 4, [VMEM, VMEM], [chunk, part, part], [mine, moving])
        image, gram = call(
            forward_kernel,
            "forward",
            12,
            [VMEM] * 4,
            [chunk, square],
            [mine, shifted(upper, "c", 1), shifted(lower, "c", 1), dense],
            2 * work,
        )
        mine_last, image, gram = lax.optimization_barrier((mine_last, image, gram))
        mine_last = added(mine_last, moving_last)
        other_last = shifted(mine_last, "c", 1)
        image, gram_mine = call(
            forward_mine_kernel, "forward_mine", 12, [VMEM] * 3, [chunk, square], [mine_last, dense, image], work
        )
        packed = call(
            forward_last_kernel,
            "forward_last",
            12,
            [VMEM] * 5,
            [packed_shape],
            [other_last, dense, image, gram, gram_mine],
            work,
        )
        halves = mine, mine_last
    gram = call(gram_kernel, "gram", 50, [VMEM], [((K // 2, 2 * K), f32)], [own])
    gram = summed_by_all(summed_by_all(gram + shifted(gram, "c", 1), PLANE), ("h", "l"))
    return call(
        finish_kernel, "finish", 50, [VMEM] * (ITERS + 1), [((ITERS, K, OWN), f32)], [gram, own, *settled]
    )


def solution(mesh):
    fine = Mesh(mesh.devices.reshape(4, 4, 4, 2, 2), BLK + ROWS)
    in_specs = (
        P(BLK, ROWS, None),
        P(None, BLK),
        P(BLK, ROWS),
        P(BLK, ROWS),
        P(BLK, ROWS),
    )
    out_specs = P(None, None, BLK + ROWS)
    return jax.shard_map(local, mesh=fine, in_specs=in_specs, out_specs=out_specs, check_vma=False)
```

```python
import jax
import jax.numpy as jnp
from jax import lax
from jax.experimental import pallas as pl
from jax.experimental.pallas import tpu as pltpu
from jax.sharding import Mesh
from jax.sharding import PartitionSpec as P

TILE = 128
K = 64
RB = 8
CB = 32
MAXB = 256
ITERS = 4
CELLS = 262144.0
WIDTH = CB * TILE
HEIGHT = RB * TILE
HALF = WIDTH // 2
OWN = WIDTH // 4
PEERS = 16
EACH = 5
PANEL = 8
START_MIB = 40
BATCHES = 8
BATCH = MAXB // BATCHES

f32 = jnp.float32
bf16 = jnp.bfloat16
BLK = ("y", "x", "h")
ROWS = ("l", "c")
PLANE = ("y", "x")
VMEM = pl.BlockSpec(memory_space=pltpu.VMEM)
SMEM = pl.BlockSpec(memory_space=pltpu.SMEM)
HBM = pl.BlockSpec(memory_space=pltpu.HBM)


def dot_rows(a, b):
    return lax.dot_general(a, b, (((1,), (1,)), ((), ())), preferred_element_type=f32)


def params(mib):
    return pltpu.CompilerParams(vmem_limit_bytes=mib << 20)


def write_packed(out, image, gram):
    for n in range(PEERS * EACH):
        rows = pl.ds((n % EACH) * 8, 8)
        if n < 64:
            g, j = divmod(n, 8)
            out[n // EACH, rows, :] = image[g * 8 : g * 8 + 8, j * TILE : (j + 1) * TILE]
        elif n < 72 and gram is not None:
            g = n - 64
            out[n // EACH, rows, :] = gram[g * 8 : g * 8 + 8, :]
        else:
            out[n // EACH, rows, :] = jnp.zeros((8, TILE), f32)


def read_packed(packed, n):
    return packed[n // EACH, pl.ds((n % EACH) * 8, 8), :]


def two_parts(x):
    high = x.astype(bf16)
    low = (x - high.astype(f32)).astype(bf16)
    return jnp.concatenate([high, low], axis=0)


def gram_of(parts):
    four = dot_rows(parts, parts)
    two = four[:K] + four[K:]
    return two[:, :K] + two[:, K:]


def reciprocal(x):
    near = pl.reciprocal(x, approx=True)
    near = near * (2.0 - x * near)
    return near * (2.0 - x * near)


def inverse_factor(gram):
    shape = (K, 2 * K)
    row = lax.broadcasted_iota(jnp.int32, shape, 0)
    col = lax.broadcasted_iota(jnp.int32, shape, 1)
    rest = jnp.concatenate([gram, (row[:, :K] == col[:, :K]).astype(f32)], axis=1)
    finished = []
    for k in range(0, K, PANEL):
        here = (K - k, 2 * K)
        below = row[: K - k]
        columns = [jnp.broadcast_to(rest[:, k + j : k + j + 1], here) for j in range(PANEL)]
        lines = [rest[j : j + 1, :] for j in range(PANEL)]
        for j in range(PANEL):
            inverse = reciprocal(columns[j][j : j + 1, :])
            factor = jnp.where(below > j, columns[j] * inverse, 0.0)
            for later in range(j + 1, PANEL):
                columns[later] = columns[later] - factor * columns[later][j : j + 1, :]
                lines[later] = lines[later] - factor[later : later + 1, :] * lines[j]
            rest = rest - factor * lines[j]
        finished.append(rest[:PANEL])
        rest = rest[PANEL:]
    work = jnp.concatenate(finished, axis=0)
    diagonal = jnp.sum(jnp.where(row == col, work, 0.0), axis=1, keepdims=True)
    return work[:, K:] * lax.rsqrt(diagonal)


def start_kernel(row_blocks, col_blocks, live, turn, tiles, basis, dense, packed, stock, first, sems, first_sem):
    get_basis = pltpu.make_async_copy(basis, first, first_sem)
    get_basis.start()
    copies = []
    for n in range(BATCHES):
        span = pl.ds(n * BATCH, BATCH)
        copies.append(pltpu.make_async_copy(tiles.at[span], stock.at[span], sems.at[n]))
        copies[-1].start()
    core, count = turn[0], live[0]

    def window(s):
        col = col_blocks[s]
        quarter = col // (CB // 4)
        position = (((quarter % 2) ^ core) * 2 + quarter // 2) * (CB // 4) + col % (CB // 4)
        return (
            pl.ds(pl.multiple_of(row_blocks[s] * TILE, TILE), TILE),
            pl.ds(pl.multiple_of(position * TILE, TILE), TILE),
        )

    def put(s, carry):
        dense[window(s)] = jnp.where(s < count, stock[s], jnp.zeros((TILE, TILE), bf16))
        return carry

    for n in range(BATCHES):
        copies[n].wait()
        lax.fori_loop(n * BATCH, (n + 1) * BATCH, put, 0, unroll=8)
    get_basis.wait()
    image = jnp.zeros((K, HEIGHT), f32)
    for p in range(4):
        q = (p % 2) * 2 + ((p // 2) ^ core)
        part = first[:, pl.ds(pl.multiple_of(q * OWN, OWN), OWN)]
        image = image + dot_rows(part, dense[:, p * OWN : (p + 1) * OWN])
    write_packed(packed, image, None)


def gathered(p, half, dense):
    parts = two_parts(half)
    image = dot_rows(parts, dense[:, p * OWN : (p + 1) * OWN])
    return image[:K] + image[K:], gram_of(parts)


def forward_kernel(mine, upper, lower, dense, image, gram):
    image_mine, gram_mine = gathered(0, mine[...], dense)
    image_other, gram_other = gathered(2, jnp.concatenate([upper[...], lower[...]], axis=0), dense)
    image[...] = image_mine + image_other
    gram[...] = gram_mine + gram_other


def forward_mine_kernel(mine, dense, image_before, image, gram):
    found, gram[...] = gathered(1, mine[...], dense)
    image[...] = image_before[...] + found


def forward_last_kernel(other, dense, image_before, gram_before, gram_mine, packed):
    found, gram_other = gathered(3, other[...], dense)
    gram = gram_before[...] + (gram_mine[...] + gram_other)
    write_packed(packed, image_before[...] + found, jnp.concatenate([gram, gram], axis=1))


def gram_kernel(own, out):
    gram = gram_of(two_parts(own[...]))
    out[...] = jnp.concatenate([gram[: K // 2], gram[K // 2 :]], axis=1)


def image_of(packed):
    return jnp.concatenate(
        [jnp.concatenate([read_packed(packed, g * 8 + j) for j in range(8)], axis=1) for g in range(8)],
        axis=0,
    )


def spread(chunk, image_half, dense, mine, other):
    for p, target in ((chunk, mine), (2 + chunk, other)):
        for n in range(2):
            width = OWN // 2
            source = pl.ds(p * OWN + n * width, width)
            product = jnp.dot(image_half, dense[:, source], preferred_element_type=f32)
            target[:, n * width : (n + 1) * width] = product


def first_backward_kernel(packed, dense, mine, other, kept):
    kept[...] = image_of(packed).astype(bf16)
    spread(0, kept[...], dense, mine, other)


def backward_kernel(packed, dense, mine, other, kept, inverse):
    gram = jnp.concatenate([read_packed(packed, 64 + g) for g in range(8)], axis=0)[:, :K]
    found = inverse_factor(gram * (1.0 / CELLS))
    inverse[...] = found
    image = jnp.dot(found, image_of(packed), precision=lax.Precision.HIGHEST, preferred_element_type=f32)
    kept[...] = image.astype(bf16)
    spread(0, kept[...], dense, mine, other)


def backward_last_kernel(kept, dense, mine, other):
    spread(1, kept[...], dense, mine, other)


def add_kernel(a, b, out):
    out[...] = a[...] + b[...]


def add_parts_kernel(a, b, out, upper, lower):
    total = a[...] + b[...]
    out[...] = total
    upper[...] = total[: K // 2]
    lower[...] = total[K // 2 :]


def share_kernel(parts, out):
    total = parts[0]
    for n in range(1, parts.shape[0]):
        total = total + parts[n]
    for n in range(out.shape[0]):
        out[n] = total


def finish_kernel(turn, gram, *refs):
    halves, last_half, inverses, out = refs[: 2 * ITERS - 2], refs[2 * ITERS - 2], refs[2 * ITERS - 1 : -1], refs[-1]
    whole = jnp.concatenate([gram[:, :K], gram[:, K:]], axis=0)
    last = inverse_factor(whole * (1.0 / CELLS))
    for i in range(ITERS):
        if i < ITERS - 1:
            found, taken = inverses[i][...], jnp.where(turn[1] == 0, halves[2 * i][...], halves[2 * i + 1][...])
        else:
            found, taken = last, last_half[...]
        out[i] = jnp.dot(found, taken, precision=lax.Precision.HIGHEST, preferred_element_type=f32)


def shifted(x, axis, by):
    count = lax.axis_size(axis)
    return lax.ppermute(x, axis, [(i, (i + by) % count) for i in range(count)])


def summed_by_all(x, axes):
    count = lax.axis_size(axes)
    return jnp.sum(lax.all_to_all(jnp.broadcast_to(x[None], (count, *x.shape)), axes, 0, 0, tiled=True), axis=0)


def call(kernel, name, mib, ins, outs, arrays, flops=0, scratch=()):
    shapes = tuple(jax.ShapeDtypeStruct(*o) for o in outs)
    moved = sum(a.size * a.dtype.itemsize for a in (*arrays, *shapes))
    found = pl.pallas_call(
        kernel,
        out_shape=shapes,
        in_specs=ins,
        out_specs=(VMEM,) * len(outs),
        scratch_shapes=list(scratch),
        compiler_params=params(mib),
        cost_estimate=pl.CostEstimate(flops=flops, bytes_accessed=moved, transcendentals=0),
        name=name,
    )(*arrays)
    return found[0] if len(outs) == 1 else found


def shared(parts, count):
    return call(share_kernel, "share", 4, [VMEM], [((count, *parts.shape[1:]), f32)], [parts])


def added(a, b):
    return call(add_kernel, "add", 4, [VMEM, VMEM], [(a.shape, f32)], [a, b])


def summed_over_blk(packed):
    shares = lax.all_to_all(packed, PLANE, 0, 0, tiled=True)
    shares = lax.all_to_all(shared(shares, 4), "h", 0, 0, tiled=True)
    return lax.all_to_all(shared(shares, PEERS), PLANE, 0, 0, tiled=True)


def local(sens_tiles, start_basis, row_blocks, col_blocks, live_counts):
    core, low = lax.axis_index("c"), lax.axis_index("l")
    turn = jnp.stack([core, low]).astype(jnp.int32)
    packed_shape = ((PEERS, EACH * 8, TILE), f32)
    chunk, square, kept_shape = ((K, OWN), f32), ((K, K), f32), ((K, HEIGHT), bf16)
    work = 2 * K * HEIGHT * HALF
    dense, packed = call(
        start_kernel,
        "start",
        START_MIB,
        [SMEM, SMEM, SMEM, SMEM, HBM, HBM],
        [((HEIGHT, WIDTH), bf16), packed_shape],
        [row_blocks.reshape(MAXB), col_blocks.reshape(MAXB), live_counts.reshape(1), turn, sens_tiles, start_basis],
        2 * work,
        [
            pltpu.VMEM(sens_tiles.shape, bf16),
            pltpu.VMEM(start_basis.shape, bf16),
            pltpu.SemaphoreType.DMA((BATCHES,)),
            pltpu.SemaphoreType.DMA,
        ],
    )
    halves, inverses = [], []
    for iteration in range(ITERS):
        packed = summed_over_blk(packed)
        if iteration == 0:
            mine, other, kept = call(first_backward_kernel, "backward", 8, [VMEM, VMEM], [chunk, chunk, kept_shape], [packed, dense], work)
        else:
            mine, other, kept, inverse = call(
                backward_kernel, "backward", 8, [VMEM, VMEM], [chunk, chunk, kept_shape, square], [packed, dense], work
            )
            inverses.append(inverse)
        moving = shifted(other, "c", 1)
        mine_last, other_last = call(backward_last_kernel, "backward_last", 8, [VMEM, VMEM], [chunk, chunk], [kept, dense], work)
        mine = added(mine, moving)
        if iteration == ITERS - 1:
            mine_last = added(mine_last, shifted(other_last, "c", 1))
            own = jnp.where(low == 0, mine, mine_last)
            sent = jnp.where(low == 0, mine_last, mine)
            own = own + shifted(sent, "l", 1)
            break
        moving = shifted(mine, "l", 1)
        mine_last = added(mine_last, shifted(other_last, "c", 1))
        moving_last = shifted(mine_last, "l", 1)
        mine, mine_last = lax.optimization_barrier((mine, mine_last))
        part = ((K // 2, OWN), f32)
        mine, upper, lower = call(add_parts_kernel, "add_parts", 4, [VMEM, VMEM], [chunk, part, part], [mine, moving])
        image, gram = call(
            forward_kernel,
            "forward",
            12,
            [VMEM] * 4,
            [chunk, square],
            [mine, shifted(upper, "c", 1), shifted(lower, "c", 1), dense],
            2 * work,
        )
        mine_last, image, gram = lax.optimization_barrier((mine_last, image, gram))
        mine_last = added(mine_last, moving_last)
        other_last = shifted(mine_last, "c", 1)
        image, gram_mine = call(
            forward_mine_kernel, "forward_mine", 12, [VMEM] * 3, [chunk, square], [mine_last, dense, image], work
        )
        packed = call(
            forward_last_kernel,
            "forward_last",
            12,
            [VMEM] * 5,
            [packed_shape],
            [other_last, dense, image, gram, gram_mine],
            work,
        )
        halves += [mine, mine_last]
    gram = call(gram_kernel, "gram", 50, [VMEM], [((K // 2, 2 * K), f32)], [own])
    gram = summed_by_all(summed_by_all(gram + shifted(gram, "c", 1), PLANE), ("h", "l"))
    return call(
        finish_kernel,
        "finish",
        50,
        [SMEM] + [VMEM] * (3 * ITERS - 1),
        [((ITERS, K, OWN), f32)],
        [turn, gram, *halves, own, *inverses],
    )


def solution(mesh):
    fine = Mesh(mesh.devices.reshape(4, 4, 4, 2, 2), BLK + ROWS)
    in_specs = (
        P(BLK, ROWS, None),
        P(None, BLK),
        P(BLK, ROWS),
        P(BLK, ROWS),
        P(BLK, ROWS),
    )
    out_specs = P(None, None, BLK + ROWS)
    return jax.shard_map(local, mesh=fine, in_specs=in_specs, out_specs=out_specs, check_vma=False)
```
